256 devices in a mesh: ugrp: 8 (over z), item: 32 (over y, x, core).
Axes of the slice: x: 4, y: 4, z: 8, core: 2. Of those that a mesh axis runs over, the one named last changes fastest.
Arguments:
- user_emb: bfloat16 [262144, 128], P(('ugrp', 'item')), may hold values from -3 to 3
- item_emb: bfloat16 [65536, 128], P('item'), may hold values from -3 to 3
- user_deg: int32 [262144], P(('ugrp', 'item')), may hold values from 64 to 255
- item_deg: int32 [65536], P('item'), may hold values from 256 to 1023
- blk_rows: int32 [8192], P(('ugrp', 'item')), may hold values from 0 to 7
- blk_slot: int32 [8192], P(('ugrp', 'item')), may hold values from 0 to 7, as said below
- fetch_cols: int32 [2048], P(('ugrp', 'item')), may hold values from 0 to 511, as said below
- blk_mask: int32 [8192, 128, 128], P(('ugrp', 'item')), may hold values 0 or 1
- samples: int32 [262144, 4], P(('ugrp', 'item')), may hold values from 0 to 1023
Outputs:
- grad_users: float32 [262144, 128], P(('ugrp', 'item'))
- grad_items: float32 [65536, 128], P('item')
The draws below stay inside these ranges and needn't reach their ends.
Inputs may be any that keep to these rules, and one draw needn't show every extreme that they name: `fetch_cols`: entries of one device's column list are distinct. At most 2 of them lie in one item shard (column blocks s * 16 to (s + 1) * 16 - 1); in every ugrp group some shard holds exactly 2 entries of every device of the group. `blk_slot`: every position of a device's column list is named by at least one of its blocks.
All inputs are finite; a program needn't handle non-finite values. No bound on the sum of `blk_mask` on one device may be relied on, other than what follows from the above.
Results may differ from the reference program's by a relative error of at most 0.003.
Values may be sent and summed in bfloat16 or wider, within the bound.
A program may use at most 64 MiB of HBM per device.

```python
import jax
import jax.numpy as jnp
from jax import lax

D = 128
BLK = 128
NEG = 3
UB_DEV = 8
IB_DEV = 16
NB = 32
FETCH = 8
CAP = 2
USERS = 262144
ITEMS = 65536
NBT = 8192
FT = 2048
N_UGRP = 8


def draw_blk_slot(key, part):
    device_count = NBT // NB
    subkeys = jax.random.split(jax.random.fold_in(key, 11), device_count)

    def single(subkey):
        first_key, second_key = jax.random.split(subkey)
        additional = jax.random.randint(first_key, (NB - FETCH,), 0, FETCH, dtype=jnp.int32)
        listed = jnp.concatenate([jnp.arange(FETCH, dtype=jnp.int32), additional])
        return listed[jax.random.permutation(second_key, NB)]
    return jax.vmap(single)(subkeys).reshape(NBT)


def draw_fetch_cols(key, part):
    shard_count = ITEMS // (IB_DEV * BLK)
    device_count = FT // FETCH
    group_count = device_count // shard_count
    slot_count = shard_count * CAP
    fullest = jax.random.randint(jax.random.fold_in(key, 21), (group_count,), 0, shard_count, dtype=jnp.int32)
    fullest = jnp.repeat(fullest, shard_count)
    subkeys = jax.random.split(jax.random.fold_in(key, 22), device_count)

    def single(subkey, target):
        order_key, shuffle_key, offset_key = jax.random.split(subkey, 3)
        ranking = jax.random.permutation(order_key, slot_count).astype(jnp.int32)
        owners = jnp.arange(slot_count, dtype=jnp.int32) // CAP
        ranking = jnp.where(owners == target, ranking - slot_count, ranking)
        chosen = jnp.argsort(ranking, stable=True)[:FETCH].astype(jnp.int32)
        chosen = chosen[jax.random.permutation(shuffle_key, FETCH)]
        offsets = jax.random.randint(offset_key, (shard_count,), 0, IB_DEV, dtype=jnp.int32)
        shard_of = chosen // CAP
        return shard_of * IB_DEV + (chosen % CAP + offsets[shard_of]) % IB_DEV
    return jax.vmap(single)(subkeys, fullest).reshape(FT)


def touch_ends(values, key, smallest, largest):
    extent = values.shape
    place = [jax.random.randint(jax.random.fold_in(key, axis), (), 0, extent[axis]) for axis in range(len(extent))]
    values = values.at[tuple(place)].set(smallest)
    longest = extent.index(max(extent))
    place[longest] = (place[longest] + 1) % extent[longest]
    return values.at[tuple(place)].set(largest)


def steps_of(rng, shape, pieces, smallest, high):
    loudness = 1.0
    for axis_at, shards_of in pieces:
        heights = jax.random.uniform(jax.random.fold_in(jax.random.fold_in(rng, 6), axis_at), (shards_of,), jnp.float32, smallest / len(pieces), high / len(pieces))
        loudness = loudness * jnp.repeat(jnp.exp(heights), shape[axis_at] // shards_of).reshape((-1,) + (1,) * (len(shape) - 1 - axis_at))
    return loudness


def noise(key, extent, deviation, most, cuts=(), held_as=jnp.bfloat16):
    array = jax.random.normal(key, extent, jnp.float32) * deviation
    if len(cuts) > 0:
        array = steps_of(key, extent, cuts, -0.22, 0.18) * array
    return jnp.clip(array, min=-most, max=most).astype(held_as)


def setup_inputs(seed: int = 0) -> dict:
    keys = jax.random.split(jax.random.key(seed), 10)
    user_emb = noise(keys[0], (USERS, D), 0.4, 3.0, ((0, 256),))
    item_emb = noise(keys[1], (ITEMS, D), 0.4, 3.0, ((0, 32),))
    user_deg = touch_ends(jax.random.randint(keys[2], (USERS,), NB * BLK // (8 * UB_DEV), NB * BLK // (2 * UB_DEV)), jax.random.fold_in(keys[2], 1), NB * BLK // (8 * UB_DEV), (NB * BLK // (2 * UB_DEV)) - 1).astype(jnp.int32)
    item_deg = touch_ends(jax.random.randint(keys[3], (ITEMS,), NB * N_UGRP * BLK // (8 * IB_DEV), NB * N_UGRP * BLK // (2 * IB_DEV)), jax.random.fold_in(keys[3], 1), NB * N_UGRP * BLK // (8 * IB_DEV), (NB * N_UGRP * BLK // (2 * IB_DEV)) - 1).astype(jnp.int32)
    blk_rows = touch_ends(jax.random.randint(keys[4], (NBT,), 0, UB_DEV), jax.random.fold_in(keys[4], 1), 0, UB_DEV - 1).astype(jnp.int32)
    blk_slot = draw_blk_slot(jax.random.fold_in(keys[9], 71), 0)
    fetch_cols = draw_fetch_cols(jax.random.fold_in(keys[9], 71), 0)
    blk_mask = touch_ends((jax.random.randint(keys[7], (NBT, BLK, BLK), 0, 4) < 1).astype(jnp.int32), jax.random.fold_in(keys[7], 1), 0, 1)
    samples = touch_ends(jax.random.randint(keys[8], (USERS, NEG + 1), 0, FETCH * BLK), jax.random.fold_in(keys[8], 1), 0, (FETCH * BLK) - 1).astype(jnp.int32)
    return {"user_emb": user_emb, "item_emb": item_emb, "user_deg": user_deg, "item_deg": item_deg, "blk_rows": blk_rows, "blk_slot": blk_slot, "fetch_cols": fetch_cols, "blk_mask": blk_mask, "samples": samples}


def reference(user_emb, item_emb, user_deg, item_deg, blk_rows, blk_slot, fetch_cols, blk_mask, samples):
    device_count = NBT // NB
    column_blocks = ITEMS // BLK
    user_scale = lax.rsqrt(user_deg.astype(jnp.float32))[:, None]
    item_scale = lax.rsqrt(item_deg.astype(jnp.float32))[:, None]
    rows_split = blk_rows.reshape(device_count, NB)
    slots_split = blk_slot.reshape(device_count, NB)
    cols_split = fetch_cols.reshape(device_count, FETCH)
    masks_split = blk_mask.reshape(device_count, NB, BLK, BLK)

    def propagate(push_users, push_items):
        push_users = lax.optimization_barrier(push_users)
        push_items = lax.optimization_barrier(push_items)
        item_tiles = push_items.reshape(column_blocks, BLK, D)
        user_tiles = push_users.reshape(device_count, UB_DEV, BLK, D)

        def device_step(running, inputs):
            row_ids, slot_ids, col_ids, tiles, own_users = inputs
            tiles_float = tiles.astype(jnp.float32)
            fetched = item_tiles[col_ids].astype(jnp.float32)[slot_ids]
            products = jnp.einsum('bij,bjd->bid', tiles_float, fetched, precision=lax.Precision.HIGHEST)
            user_sum = jax.ops.segment_sum(products, row_ids, num_segments=UB_DEV)
            needed = own_users[row_ids].astype(jnp.float32)
            backward = jnp.einsum('bji,bjd->bid', tiles_float, needed, precision=lax.Precision.HIGHEST)
            column_terms = jax.ops.segment_sum(backward, slot_ids, num_segments=FETCH).astype(jnp.bfloat16)
            column_terms = lax.optimization_barrier(column_terms)
            running = running.at[col_ids].add(column_terms.astype(jnp.float32))
            return (running, user_sum)
        start = jnp.zeros((column_blocks, BLK, D), jnp.float32)
        running, user_sums = lax.scan(device_step, start, (rows_split, slots_split, cols_split, masks_split, user_tiles))
        return (user_sums.reshape(USERS, D), running.reshape(ITEMS, D))

    def layer(user_now, item_now):
        push_users = (user_scale * user_now).astype(jnp.bfloat16)
        push_items = (item_scale * item_now).astype(jnp.bfloat16)
        user_part, item_part = propagate(push_users, push_items)
        return (user_scale * user_part, item_scale * item_part)
    user_zero = user_emb.astype(jnp.float32)
    item_zero = item_emb.astype(jnp.float32)
    user_one, item_one = layer(user_zero, item_zero)
    user_two, item_two = layer(user_one, item_one)
    user_final = (user_zero + user_one + user_two) / 3.0
    item_final = (item_zero + item_one + item_two) / 3.0
    item_sent = lax.optimization_barrier(item_final.astype(jnp.bfloat16)).reshape(column_blocks, BLK, D)
    sample_count = samples.shape[1]
    finals_split = user_final.reshape(device_count, UB_DEV * BLK, D)
    samples_split = samples.reshape(device_count, UB_DEV * BLK, sample_count)

    def loss_one(inputs):
        own_final, own_samples, col_ids = inputs
        flattened = item_sent[col_ids].reshape(FETCH * BLK, D)
        picked = flattened[own_samples].astype(jnp.float32)
        scores = lax.optimization_barrier(jnp.sum(own_final[:, None, :] * picked, axis=2))
        exponent = jnp.exp(scores)
        softmax_rows = exponent / lax.optimization_barrier(jnp.sum(exponent, axis=1, keepdims=True))
        positive = (jnp.arange(sample_count, dtype=jnp.int32) == 0).astype(jnp.float32)
        slopes = softmax_rows - positive[None, :]
        user_grad = lax.optimization_barrier(jnp.sum(slopes[:, :, None] * picked, axis=1))
        spread = (slopes[:, :, None] * own_final[:, None, :]).reshape(-1, D)
        sample_terms = jax.ops.segment_sum(spread, own_samples.reshape(-1), num_segments=FETCH * BLK).astype(jnp.bfloat16)
        return (user_grad, sample_terms)
    user_grads, sample_terms = lax.map(loss_one, (finals_split, samples_split, cols_split))
    sample_terms = lax.optimization_barrier(sample_terms)
    global_rows = (cols_split[:, :, None] * BLK + jnp.arange(BLK, dtype=jnp.int32)[None, None, :]).reshape(-1)
    item_grad_final = jnp.zeros((ITEMS, D), jnp.float32).at[global_rows].add(sample_terms.reshape(-1, D).astype(jnp.float32))
    user_down = user_grads.reshape(USERS, D) / 3.0
    item_down = item_grad_final / 3.0
    first_user, first_item = layer(user_down, item_down)
    second_user, second_item = layer(first_user, first_item)
    return (user_down + first_user + second_user, item_down + first_item + second_item)
```

```python
import jax
import jax.numpy as jnp
from jax import lax
from jax.experimental import pallas as pl
from jax.experimental.pallas import tpu as pltpu
from jax.sharding import PartitionSpec as P

F32, BF16, I32 = jnp.float32, jnp.bfloat16, jnp.int32
MESH = pl.DeviceIdType.MESH
NT = (((1,), (1,)), ((), ()))
NZ, NC, PEERS = 8, 2, 16
RS_TYPES = (BF16, BF16, BF16, BF16, BF16)


def place_kernel(rows, slots, mask, out):
    out[...] = jnp.zeros_like(out)

    @pl.loop(0, mask.shape[0])
    def _(b):
        at = (
            pl.ds(pl.multiple_of(rows[b] * 128, 128), 128),
            pl.ds(pl.multiple_of(slots[b] * 128, 128), 128),
        )
        out[at] = (out[at].astype(F32) + mask[b].astype(F32)).astype(BF16)


def main_kernel(
    cols, uemb, iemb, udeg, ideg, picks, mat,
    gu_out, gi_out,
    u0, scale_u, i0, scale_i, ufin, gu, gsum, isum,
    oh, picked, sel, selt, tables, zs, zr, cs, cr, xs, xr, ds, dr, relay, wide,
    pf, pa, sb0, sb1, sb2, sb3, sb4, sa0, sa1, sa2, sa3, sa4,
    rb0, rb1, rb2, rb3, rb4, ra0, ra1, ra2, ra3, ra4,
    early_s, early_r, late_s, late_r,
    z_send, z_recv, c_sem, x_sem, d_sem, ag_send, ag_recv, rs_send, rs_recv, o_sem,
):
    sb, sa = (sb0, sb1, sb2, sb3, sb4), (sa0, sa1, sa2, sa3, sa4)
    rb, ra = (rb0, rb1, rb2, rb3, rb4), (ra0, ra1, ra2, ra3, ra4)
    z, j = lax.axis_index("ugrp"), lax.axis_index("item")
    c = j % 2
    chip = j // 2
    x, y = chip % 4, chip // 4
    nc = 1 - c
    a, b = x * nc + y * c, y * nc + x * c
    me = z * 2 + c

    def plane(a_to, b_to):
        return (z, ((b_to * nc + a_to * c) * 4 + a_to * nc + b_to * c) * 2 + c)

    up_a, down_a = plane((a + 1) % 4, b), plane((a + 3) % 4, b)
    up_b, down_b = plane(a, (b + 1) % 4), plane(a, (b + 3) % 4)

    def column(k):
        z_to, c_to = (z + k // 2) % NZ, (c + k % 2) % NC
        return (z_to, chip * 2 + c_to), z_to * 2 + c_to

    def remote(src, dst, send, recv, to):
        pltpu.make_async_remote_copy(
            src_ref=src, dst_ref=dst, send_sem=send, recv_sem=recv, device_id=to, device_id_type=MESH
        ).start()

    def await_bytes(ref, sem):
        pltpu.make_async_copy(ref, ref, sem).wait()

    barrier = pltpu.get_barrier_semaphore()
    for to in (up_a, down_a, up_b, down_b):
        pl.semaphore_signal(barrier, inc=1, device_id=to, device_id_type=MESH)

    @pl.loop(1, PEERS)
    def _(k):
        to, _ = column(k)
        pl.semaphore_signal(barrier, inc=1, device_id=to, device_id_type=MESH)

    def z_start(n):
        own = pltpu.make_async_copy(zs.at[n, me], zr.at[n, me], z_recv.at[n])
        own.start()

        @pl.loop(1, PEERS)
        def _(k):
            to, slot = column(k)
            remote(zs.at[n, slot], zr.at[n, me], z_send.at[n], z_recv.at[n], to)

    def z_wait(n):
        await_bytes(zr.at[n], z_recv.at[n])

    def at(b_off, a_off, lo=0, rows=32):
        return pl.ds((b_off * 4 + a_off) * 32 + lo, rows)

    def ag_copy(n, src, dst, slot, to):
        remote(tables.at[n, src], tables.at[n, dst], ag_send.at[n], ag_recv.at[n, slot], to)

    def ag_wait(n, slot, rows=32):
        await_bytes(tables.at[n, pl.ds(0, rows)], ag_recv.at[n, slot])

    def ag_along_b(n, a_off):
        ag_copy(n, at(0, a_off), at(3, a_off), 12 + a_off, up_b)
        ag_copy(n, at(0, a_off), at(1, a_off), 4 + a_off, down_b)

    def ag_start(n):
        ag_copy(n, at(0, 0), at(0, 3), 3, up_a)
        ag_copy(n, at(0, 0), at(0, 1), 1, down_a)
        ag_along_b(n, 0)

    def ag_mid1(n):
        ag_wait(n, 3)
        ag_copy(n, at(0, 3, 0, 16), at(0, 2, 0, 16), 2, up_a)
        ag_wait(n, 1)
        ag_copy(n, at(0, 1, 16, 16), at(0, 2, 16, 16), 0, down_a)
        ag_along_b(n, 3)
        ag_along_b(n, 1)

    def ag_mid2(n):
        ag_wait(n, 2, 16)
        ag_wait(n, 0, 16)
        ag_along_b(n, 2)
        ag_wait(n, 12)
        ag_copy(n, at(3, 0), at(2, 0), 8, up_b)
        ag_wait(n, 7)
        ag_wait(n, 5)
        ag_copy(n, at(1, 1), at(2, 1), 9, down_b)
        ag_wait(n, 15)
        ag_copy(n, at(3, 3), at(2, 3), 11, up_b)
        ag_wait(n, 6)
        ag_copy(n, at(1, 2), at(2, 2), 10, down_b)

    def ag_end(n):
        for slot in (4, 13, 14, 8, 9, 10, 11):
            ag_wait(n, slot)

    def ring_start(n, half, buf, got, stage, up, down):
        pairs = ((2 * half * 2, up), (2 * half * 2 + half, down), (3 * half, up), (6 * half, down))
        for slot, (row, to) in enumerate(pairs):
            remote(
                buf.at[pl.ds(row, half)], got.at[slot],
                rs_send.at[n, stage], rs_recv.at[n, stage * 6 + slot], to,
            )

    def ring_mid(n, half, part, buf, got, stage, up, down):
        for slot, (row, to) in enumerate(((2 * half, up), (7 * half, down))):
            rows = pl.ds(row, half)
            await_bytes(got.at[slot], rs_recv.at[n, stage * 6 + slot])
            buf[rows, :] = (part[rows, :] + got[slot].astype(F32)).astype(buf.dtype)
            remote(
                buf.at[rows], got.at[4 + slot],
                rs_send.at[n, stage], rs_recv.at[n, stage * 6 + 4 + slot], to,
            )

    def ring_end(n, half, part, got, stage):
        for slot in (2, 3, 4, 5):
            await_bytes(got.at[slot], rs_recv.at[n, stage * 6 + slot])
        low = part[pl.ds(0, half), :] + got[3].astype(F32) + got[4].astype(F32)
        high = part[pl.ds(half, half), :] + got[2].astype(F32) + got[5].astype(F32)
        return low, high

    def rs_start(n, zn):
        z_wait(zn)
        got = zr[zn].astype(F32)
        stack = relay.reshape(16, 8, 8, 128)
        for h in range(2):
            for f in range(4):
                stack[:, h * 4 + f, :, :] = got[:, h * 8 : h * 8 + 8, f * 128 : f * 128 + 128]
        terms = jnp.concatenate(
            [relay[pl.ds(f, 128, stride=8), :] for f in range(8)], axis=1
        ).astype(BF16)
        for g in (2, 1, 3, 0):
            rows = pl.ds(g * 128, 128)
            part = jnp.dot(selt[rows, :], terms, preferred_element_type=F32)
            pf[n % 2, rows, :] = part
            if g:
                sb[n][rows, :] = part.astype(sb[n].dtype)
        ring_start(n, 64, sb[n], rb[n], 0, up_b, down_b)

    def rs_b2(n):
        ring_mid(n, 64, pf.at[n % 2], sb[n], rb[n], 0, up_b, down_b)

    def rs_a1(n):
        for i, half in enumerate(ring_end(n, 64, pf.at[n % 2], rb[n], 0)):
            rows = pl.ds(i * 64, 64)
            pa[n % 2, rows, :] = half
            sa[n][rows, :] = half.astype(sa[n].dtype)
        ring_start(n, 16, sa[n], ra[n], 1, up_a, down_a)

    def rs_a2(n):
        ring_mid(n, 16, pa.at[n % 2], sa[n], ra[n], 1, up_a, down_a)

    def rs_end(n):
        return jnp.concatenate(ring_end(n, 16, pa.at[n % 2], ra[n], 1), axis=0)

    def send_terms(zn, terms):
        parts = terms.reshape(16, 8, 1024)
        zs[zn] = jnp.concatenate([parts[:, :, :512], parts[:, :, 512:]], axis=1).astype(BF16)
        z_start(zn)

    def send_picks(zn, n):
        found = jnp.dot(sel[...], tables[n], preferred_element_type=F32)
        for f in range(8):
            relay[pl.ds(f, 128, stride=8), :] = found[:, f * 128 : f * 128 + 128]
        stack = relay.reshape(16, 8, 8, 128)
        halves = [
            jnp.concatenate([stack[:, h * 4 + f, :, :] for f in range(4)], axis=2)
            for h in range(2)
        ]
        zs[zn] = jnp.concatenate(halves, axis=1).astype(BF16)
        z_start(zn)

    def fetched(zn):
        z_wait(zn)
        got = zr[zn].astype(F32)
        return jnp.concatenate(
            [got[:, :8, :].reshape(128, 512), got[:, 8:, :].reshape(128, 512)], axis=1
        ).astype(BF16)

    def to_users(rows):
        return lax.dot_general(rows, mat[...], NT, preferred_element_type=F32)

    def to_columns(rows):
        return jnp.dot(rows, mat[...], preferred_element_type=F32)

    def push_items(n, rows):
        tables[n, pl.ds(0, 32), :] = (scale_i[...] * rows).astype(BF16)
        ag_start(n)

    def build_picks(k):
        line = picks[pl.ds(k, 1), :]

        @pl.loop(0, 8)
        def _(r):
            at_row = pl.multiple_of(r * 128, 128)
            number = lax.broadcasted_iota(I32, (128, 1024), 0) + at_row
            oh[k, pl.ds(at_row, 128), :] = jnp.where(number == line, 1.0, 0.0).astype(BF16)

    sub = lax.broadcasted_iota(I32, (8, 128), 0)
    want = jnp.zeros((8, 128), I32)
    for f in range(8):
        want = jnp.where(sub == f, cols[f], want)
    cs[...] = want
    cr[me] = want
    lane = lax.broadcasted_iota(I32, (16, 128), 1)
    row = lax.broadcasted_iota(I32, (16, 128), 0)
    feature = jnp.where(row < 8, me * 8 + row, (z * 2 + nc) * 8 + row - 8)
    some = lax.dot_general(
        jnp.where(lane == feature, 1.0, 0.0).astype(BF16), iemb[...], NT, preferred_element_type=F32
    )
    for blk in range(16):
        cut = some[:, blk * 128 : blk * 128 + 128]
        relay[pl.ds(blk * 8, 8), :] = cut[:8]
        relay[pl.ds(128 + blk * 8, 8), :] = cut[8:]
    mine, theirs = (
        jnp.concatenate([relay[pl.ds(first + f, 16, stride=8), :] for f in range(8)], axis=1)
        for first in (0, 128)
    )
    i0[pl.ds(0, 16), :] = mine
    xs[...] = theirs.astype(BF16)
    ds[...] = lax.rsqrt(ideg[...].astype(F32))

    pl.semaphore_wait(barrier, 4 + PEERS - 1)

    sibling = (z, chip * 2 + nc)
    remote(xs, xr, x_sem.at[0], x_sem.at[1], sibling)
    remote(ds, dr, d_sem.at[0], d_sem.at[1], sibling)

    @pl.loop(1, PEERS)
    def _(k):
        to, _ = column(k)
        remote(cs, cr.at[me], c_sem.at[0], c_sem.at[1], to)

    eye = jnp.where(
        lax.broadcasted_iota(I32, (128, 128), 0) == lax.broadcasted_iota(I32, (128, 128), 1), 1.0, 0.0
    ).astype(BF16)
    user_rows = lax.dot_general(eye, uemb[...], NT, preferred_element_type=F32)
    u0[...] = user_rows
    scale_u[...] = lax.rsqrt(udeg[...].astype(F32))
    send_terms(0, to_columns((scale_u[...] * user_rows).astype(BF16)))

    await_bytes(xr, x_sem.at[1])
    await_bytes(dr, d_sem.at[1])
    i0[pl.ds(16, 16), :] = xr[...].astype(F32)
    scale_i[pl.ds(0, 16), :] = jnp.concatenate([ds[...]] * 8, axis=1)
    scale_i[pl.ds(16, 16), :] = jnp.concatenate([dr[...]] * 8, axis=1)
    push_items(0, i0[...])

    await_bytes(cr.at[pl.ds(0, PEERS - 1)], c_sem.at[1])
    col = cr[...].reshape(128, 128)
    chip_of = lax.shift_right_logical(col, jnp.full_like(col, 5))
    x_of, y_of = chip_of & 3, lax.shift_right_logical(chip_of, jnp.full_like(col, 2))
    a_of, b_of = x_of * nc + y_of * c, y_of * nc + x_of * c
    spot = (((b_of - b + 4) & 3) * 4 + ((a_of - a + 4) & 3)) * 32 + ((col + 16 * c) & 31)
    spot_t = spot.astype(F32).T
    for q in range(4):
        sel[:, q * 128 : q * 128 + 128] = jnp.where(
            spot == lax.broadcasted_iota(I32, (128, 128), 1) + q * 128, 1.0, 0.0
        ).astype(BF16)
        selt[pl.ds(q * 128, 128), :] = jnp.where(
            spot_t == (lax.broadcasted_iota(I32, (128, 128), 0) + q * 128).astype(F32), 1.0, 0.0
        ).astype(BF16)

    ag_mid1(0)
    rs_start(0, 0)
    ag_mid2(0)
    rs_b2(0)
    ag_end(0)
    send_picks(1, 0)
    rs_a1(0)
    build_picks(0)
    rs_a2(0)
    item_one = scale_i[...] * rs_end(0)
    isum[...] = i0[...] + item_one
    push_items(1, item_one)

    user_one = scale_u[...] * to_users(fetched(1))
    ufin[...] = u0[...] + user_one
    send_terms(2, to_columns((scale_u[...] * user_one).astype(BF16)))

    ag_mid1(1)
    build_picks(1)
    ag_mid2(1)
    rs_start(1, 2)
    ag_end(1)
    send_picks(3, 1)
    rs_b2(1)
    build_picks(2)
    rs_a1(1)
    rs_a2(1)
    item_final = (isum[...] + scale_i[...] * rs_end(1)) / 3.0
    tables[2, pl.ds(0, 32), :] = item_final.astype(BF16)
    ag_start(2)
    user_two = scale_u[...] * to_users(fetched(3))
    ufin[...] = (ufin[...] + user_two) / 3.0
    ag_mid1(2)
    build_picks(3)
    ag_mid2(2)
    ag_end(2)
    send_picks(4, 2)

    final = fetched(4)
    exps = []
    for k in range(4):
        rows = jnp.dot(final, oh[k], preferred_element_type=F32)
        picked[k] = rows
        exps.append(jnp.exp(jnp.sum(ufin[...] * rows, axis=0, keepdims=True)))
    total = exps[0] + exps[1] + exps[2] + exps[3]
    slopes = [e / total - (1.0 if k == 0 else 0.0) for k, e in enumerate(exps)]
    spread = jnp.zeros((256, 1024), F32)
    for k in range(4):
        exact = slopes[k] * ufin[...]
        high = exact.astype(BF16)
        low = (exact - high.astype(F32)).astype(BF16)
        spread = spread + lax.dot_general(
            jnp.concatenate([high, low], axis=0), oh[k], NT, preferred_element_type=F32
        )
    send_terms(5, spread[:128] + spread[128:])
    grad = slopes[0] * picked[0]
    for k in range(1, 4):
        grad = grad + slopes[k] * picked[k]
    grad = grad / 3.0
    gu[...] = grad
    send_terms(6, to_columns((scale_u[...] * grad).astype(BF16)))

    rs_start(2, 5)
    rs_b2(2)
    rs_start(3, 6)
    rs_a1(2)
    rs_b2(3)
    rs_a2(2)
    item_down = rs_end(2) / 3.0
    push_items(3, item_down)
    rs_a1(3)
    ag_mid1(3)
    rs_a2(3)
    ag_mid2(3)
    first_item = scale_i[...] * rs_end(3)
    push_items(4, first_item)
    early_s[...] = item_down + first_item
    ag_end(3)
    send_picks(7, 3)
    ag_mid1(4)
    ag_mid2(4)
    first_user = scale_u[...] * to_users(fetched(7))
    send_terms(8, to_columns((scale_u[...] * first_user).astype(BF16)))
    gu[...] = gu[...] + first_user
    ag_end(4)
    send_picks(9, 4)

    def out_start(src, dst, sem):
        own = pltpu.make_async_copy(src.at[pl.ds(0, 16)], dst.at[me], o_sem.at[sem + 1])
        own.start()

        @pl.loop(1, PEERS)
        def _(k):
            to, _ = column(k)
            first = pl.multiple_of((k % 2) * 16, 16)
            remote(src.at[pl.ds(first, 16)], dst.at[me], o_sem.at[sem], o_sem.at[sem + 1], to)

    rs_start(4, 8)
    out_start(early_s, early_r, 0)
    rs_b2(4)
    rs_a1(4)
    rs_a2(4)
    late_s[...] = (scale_i[...] * rs_end(4)).astype(BF16)
    out_start(late_s, late_r, 2)
    second_user = scale_u[...] * to_users(fetched(9))
    gu_out[...] = (gu[...] + second_user).T
    await_bytes(early_r, o_sem.at[1])
    await_bytes(late_r, o_sem.at[3])

    @pl.loop(0, PEERS)
    def _(p):
        rows = early_r[p] + late_r[p].astype(F32)
        for f in range(8):
            wide[pl.ds(p * 8 + f, 16, stride=128), :] = rows[:, f * 128 : f * 128 + 128]

    @pl.loop(0, 16)
    def _(blk):
        rows = pl.ds(pl.multiple_of(blk * 128, 128), 128)
        gi_out[rows, :] = wide[rows, :].T

    await_bytes(xs, x_sem.at[0])
    await_bytes(ds, d_sem.at[0])
    await_bytes(cr.at[pl.ds(0, PEERS - 1)], c_sem.at[0])
    await_bytes(early_r.at[pl.ds(0, PEERS - 1)], o_sem.at[0])
    await_bytes(late_r.at[pl.ds(0, PEERS - 1)], o_sem.at[2])
    for n in range(10):
        await_bytes(zs.at[n, pl.ds(0, PEERS - 1)], z_send.at[n])
    for n in range(5):
        await_bytes(tables.at[n, pl.ds(0, 480)], ag_send.at[n])
        await_bytes(rb[n], rs_send.at[n, 0])
        await_bytes(ra[n], rs_send.at[n, 1])


def on_device(
    user_emb, item_emb, user_deg, item_deg, blk_rows, blk_slot, fetch_cols, blk_mask, samples
):
    mat = pl.pallas_call(
        place_kernel,
        out_shape=jax.ShapeDtypeStruct((1024, 1024), BF16),
        in_specs=[
            pl.BlockSpec(memory_space=pltpu.SMEM),
            pl.BlockSpec(memory_space=pltpu.SMEM),
            pl.BlockSpec(memory_space=pltpu.VMEM),
        ],
        out_specs=pl.BlockSpec(memory_space=pltpu.VMEM),
        compiler_params=pltpu.CompilerParams(vmem_limit_bytes=16 * 2**20),
        name="place_blocks",
    )(blk_rows, blk_slot, blk_mask)
    vmem = pl.BlockSpec(memory_space=pltpu.VMEM)
    dma = pltpu.SemaphoreType.DMA
    state = pltpu.VMEM((32, 1024), F32)
    users = pltpu.VMEM((128, 1024), F32)
    return pl.pallas_call(
        main_kernel,
        out_shape=(
            jax.ShapeDtypeStruct((1024, 128), F32),
            jax.ShapeDtypeStruct((2048, 128), F32),
        ),
        in_specs=[pl.BlockSpec(memory_space=pltpu.SMEM)] + [vmem] * 6,
        out_specs=(vmem, vmem),
        scratch_shapes=[
            users, pltpu.VMEM((1, 1024), F32), state, state, users, users, state, state,
            pltpu.VMEM((4, 1024, 1024), BF16), pltpu.VMEM((4, 128, 1024), F32),
            pltpu.VMEM((128, 512), BF16), pltpu.VMEM((512, 128), BF16),
            pltpu.VMEM((5, 512, 1024), BF16),
            pltpu.VMEM((10, PEERS, 16, 512), BF16), pltpu.VMEM((10, PEERS, 16, 512), BF16),
            pltpu.VMEM((8, 128), I32), pltpu.VMEM((PEERS, 8, 128), I32),
            pltpu.VMEM((16, 1024), BF16), pltpu.VMEM((16, 1024), BF16),
            pltpu.VMEM((16, 128), F32), pltpu.VMEM((16, 128), F32),
            pltpu.VMEM((1024, 128), F32), pltpu.VMEM((2048, 128), F32),
            pltpu.VMEM((2, 512, 1024), F32), pltpu.VMEM((2, 128, 1024), F32),
            *[pltpu.VMEM((512, 1024), t) for t in RS_TYPES],
            *[pltpu.VMEM((128, 1024), t) for t in RS_TYPES],
            *[pltpu.VMEM((6, 64, 1024), t) for t in RS_TYPES],
            *[pltpu.VMEM((6, 16, 1024), t) for t in RS_TYPES],
            state, pltpu.VMEM((PEERS, 16, 1024), F32),
            pltpu.VMEM((32, 1024), BF16), pltpu.VMEM((PEERS, 16, 1024), BF16),
            dma((10,)), dma((10,)), dma((2,)), dma((2,)), dma((2,)),
            dma((5,)), dma((5, 16)), dma((5, 2)), dma((5, 12)), dma((4,)),
        ],
        compiler_params=pltpu.CompilerParams(
            collective_id=0, has_side_effects=True, vmem_limit_bytes=56 * 2**20
        ),
        name="gcn",
    )(
        fetch_cols, user_emb, item_emb, user_deg.reshape(1, -1), item_deg.reshape(16, 128),
        samples.T, mat,
    )


def solution(mesh):
    both = ("ugrp", "item")
    return jax.shard_map(
        on_device,
        mesh=mesh,
        in_specs=(
            P(both, None), P("item", None), P(both), P("item"), P(both), P(both), P(both),
            P(both, None, None), P(both, None),
        ),
        out_specs=(P(both, None), P("item", None)),
        check_vma=False,
    )
```

```python
import jax
import jax.numpy as jnp
from jax import lax
from jax.experimental import pallas as pl
from jax.experimental.pallas import tpu as pltpu
from jax.sharding import PartitionSpec as P

F32, BF16, I32 = jnp.float32, jnp.bfloat16, jnp.int32
MESH = pl.DeviceIdType.MESH
NT = (((1,), (1,)), ((), ()))
NZ, PEERS, NEAR = 8, 64, 8
RS_TYPES = (BF16, BF16, F32, BF16, BF16)


def place_kernel(rows, slots, mask, out):
    out[...] = jnp.zeros_like(out)

    @pl.loop(0, mask.shape[0])
    def _(b):
        at = (
            pl.ds(pl.multiple_of(rows[b] * 128, 128), 128),
            pl.ds(pl.multiple_of(slots[b] * 128, 128), 128),
        )
        out[at] = (out[at].astype(F32) + mask[b].astype(F32)).astype(BF16)


def main_kernel(
    cols, uemb, iemb, udeg, ideg, picks, mat,
    gu_out, gi_out,
    u0, scale_u, i0, scale_i, ufin, gu, gi, isum,
    oh, picked, sel, selt, tables, zs, zr, cs, cr, xs, xr, ds, dr, relay, wide,
    pf, sb0, sb1, sb2, sb3, sb4, rb0, rb1, rb2, rb3, rb4, out_s, out_r,
    z_send, z_recv, c_sem, x_sem, d_sem, ag_send, ag_recv, rs_send, rs_recv, o_sem,
):
    sb, rb = (sb0, sb1, sb2, sb3, sb4), (rb0, rb1, rb2, rb3, rb4)
    z, j = lax.axis_index("ugrp"), lax.axis_index("item")
    c = j % 2
    x, y = (j // 2) % 4, j // 8
    near = x * 2 + c
    me = z * NEAR + near

    def along_y(d):
        return (z, ((y + d) % 4) * 8 + near)

    def nearby(k):
        n_to = ((x + k // 2) % 4) * 2 + (c + k % 2) % 2
        return (z, y * 8 + n_to), n_to

    def peer(k):
        i = k // NEAR
        z_to = (z + 4 + ((i + 1) // 2) * (1 - 2 * (i % 2))) % NZ
        (_, j_to), n_to = nearby(NEAR - 1 - k % NEAR)
        return (z_to, j_to), z_to * NEAR + n_to, n_to

    def remote(src, dst, send, recv, to):
        pltpu.make_async_remote_copy(
            src_ref=src, dst_ref=dst, send_sem=send, recv_sem=recv, device_id=to, device_id_type=MESH
        ).start()

    def await_bytes(ref, sem):
        pltpu.make_async_copy(ref, ref, sem).wait()

    barrier = pltpu.get_barrier_semaphore()
    for d in (1, 2, 3):
        pl.semaphore_signal(barrier, inc=1, device_id=along_y(d), device_id_type=MESH)

    @pl.loop(0, PEERS - 1)
    def _(k):
        pl.semaphore_signal(barrier, inc=1, device_id=peer(k)[0], device_id_type=MESH)

    def z_start(n):
        own = pltpu.make_async_copy(zs.at[n, me], zr.at[n, me], z_recv.at[n])
        own.start()

        @pl.loop(0, PEERS - 1)
        def _(k):
            to, slot, _ = peer(k)
            remote(zs.at[n, slot], zr.at[n, me], z_send.at[n], z_recv.at[n], to)

    def z_wait(n):
        await_bytes(zr.at[n], z_recv.at[n])

    def ag_start(n):
        for d in (2, 1, 3):
            remote(
                tables.at[n, pl.ds(0, 128)], tables.at[n, pl.ds((4 - d) * 128, 128)],
                ag_send.at[n], ag_recv.at[n], along_y(d),
            )

    def ag_wait(n):
        await_bytes(tables.at[n, pl.ds(128, 384)], ag_recv.at[n])

    def rs_start(n, zn):
        z_wait(zn)
        got = zr[zn].astype(F32)
        terms = jnp.concatenate(
            [got[:, :8].reshape(512, 128), got[:, 8:].reshape(512, 128)], axis=1
        ).astype(BF16)
        for d in (2, 1, 3, 0):
            part = jnp.dot(selt[pl.ds(d * 128, 128), :], terms, preferred_element_type=F32)
            if d:
                sb[n][d - 1] = part.astype(sb[n].dtype)
                remote(sb[n].at[d - 1], rb[n].at[d - 1], rs_send.at[n], rs_recv.at[n], along_y(d))
            else:
                pf[n % 2] = part

    def rs_end(n):
        await_bytes(rb[n], rs_recv.at[n])
        return pf[n % 2] + rb[n][0].astype(F32) + rb[n][1].astype(F32) + rb[n][2].astype(F32)

    def send_terms(zn, terms):
        for f in range(8):
            relay[pl.ds(f, 128, stride=8), :] = terms[:, f * 128 : f * 128 + 128]
        zs[zn] = relay[...].reshape(PEERS, 16, 128).astype(BF16)
        z_start(zn)

    def send_picks(zn, n):
        ag_wait(n)
        found = jnp.dot(sel[...], tables[n], preferred_element_type=F32)
        zs[zn] = jnp.concatenate(
            [found[:, :128].reshape(PEERS, 8, 128), found[:, 128:].reshape(PEERS, 8, 128)], axis=1
        ).astype(BF16)
        z_start(zn)

    def fetched(zn):
        z_wait(zn)
        relay[...] = zr[zn].astype(F32).reshape(1024, 128)
        return jnp.concatenate(
            [relay[pl.ds(f, 128, stride=8), :] for f in range(8)], axis=1
        ).astype(BF16)

    def to_users(rows):
        return lax.dot_general(rows, mat[...], NT, preferred_element_type=F32)

    def to_columns(rows):
        return jnp.dot(rows, mat[...], preferred_element_type=F32)

    def push_items(n, rows):
        tables[n, pl.ds(0, 128), :] = (scale_i[...] * rows).astype(BF16)
        ag_start(n)

    def build_picks(k):
        line = picks[pl.ds(k, 1), :]

        @pl.loop(0, 8)
        def _(r):
            at_row = pl.multiple_of(r * 128, 128)
            number = lax.broadcasted_iota(I32, (128, 1024), 0) + at_row
            oh[k, pl.ds(at_row, 128), :] = jnp.where(number == line, 1.0, 0.0).astype(BF16)

    lane_row = lax.broadcasted_iota(I32, (1, 128), 1) & 7
    want = jnp.zeros((1, 128), I32)
    for f in range(8):
        want = jnp.where(lane_row == f, cols[f], want)
    cs[...] = want
    cr[me] = want
    lane = lax.broadcasted_iota(I32, (16, 128), 1)
    row = lax.broadcasted_iota(I32, (16, 128), 0)
    some = lax.dot_general(
        jnp.where(lane == z * 16 + row, 1.0, 0.0).astype(BF16), iemb[...], NT,
        preferred_element_type=F32,
    )
    for blk in range(16):
        relay[pl.ds(blk * 16, 16), :] = some[:, blk * 128 : blk * 128 + 128]
    for q in range(NEAR):
        xs[q] = jnp.concatenate(
            [relay[pl.ds(q * 2 + e, 16, stride=16), :] for e in range(2)], axis=1
        ).astype(BF16)
    ds[...] = lax.rsqrt(ideg[...].astype(F32))

    pl.semaphore_wait(barrier, 3 + PEERS - 1)

    own_x = pltpu.make_async_copy(xs.at[near], xr.at[near], x_sem.at[1])
    own_x.start()
    own_d = pltpu.make_async_copy(ds, dr.at[near], d_sem.at[1])
    own_d.start()

    @pl.loop(1, NEAR)
    def _(k):
        to, n_to = nearby(k)
        remote(xs.at[n_to], xr.at[near], x_sem.at[0], x_sem.at[1], to)
        remote(ds, dr.at[near], d_sem.at[0], d_sem.at[1], to)

    @pl.loop(0, PEERS - 1)
    def _(k):
        remote(cs, cr.at[me], c_sem.at[0], c_sem.at[1], peer(k)[0])

    eye = jnp.where(
        lax.broadcasted_iota(I32, (128, 128), 0) == lax.broadcasted_iota(I32, (128, 128), 1), 1.0, 0.0
    ).astype(BF16)
    user_rows = lax.dot_general(eye, uemb[...], NT, preferred_element_type=F32)
    u0[...] = user_rows
    scale_u[...] = lax.rsqrt(udeg[...].astype(F32))
    send_terms(0, to_columns((scale_u[...] * user_rows).astype(BF16)))

    await_bytes(xr, x_sem.at[1])
    await_bytes(dr, d_sem.at[1])
    i0[...] = xr[...].astype(F32).reshape(128, 256)
    one_scale = dr[...].reshape(128, 128)
    scale_i[...] = jnp.concatenate([one_scale, one_scale], axis=1)
    push_items(0, i0[...])

    await_bytes(cr.at[pl.ds(0, PEERS - 1)], c_sem.at[1])
    col = cr[...]
    y_of = lax.shift_right_logical(col, jnp.full_like(col, 7))
    place = (((y_of - y + 4) & 3) * 128 + (col & 127)).astype(F32)
    mine = (lax.broadcasted_iota(I32, (8, 128), 1) & 7) == lax.broadcasted_iota(I32, (8, 128), 0)
    spot = jnp.sum(
        jnp.where(mine[None], jnp.broadcast_to(place, (PEERS, 8, 128)), 0.0), axis=2, keepdims=True
    ) * (1.0 / 16.0)
    spot = jnp.broadcast_to(spot, (PEERS, 8, 128)).reshape(512, 128)
    for q in range(4):
        sel[:, q * 128 : q * 128 + 128] = jnp.where(
            spot == (lax.broadcasted_iota(I32, (512, 128), 1) + q * 128).astype(F32), 1.0, 0.0
        ).astype(BF16)
        turned = spot[q * 128 : q * 128 + 128].T
        for p in range(4):
            selt[p * 128 : p * 128 + 128, q * 128 : q * 128 + 128] = jnp.where(
                turned == (lax.broadcasted_iota(I32, (128, 128), 0) + p * 128).astype(F32), 1.0, 0.0
            ).astype(BF16)

    send_picks(1, 0)
    rs_start(0, 0)
    build_picks(0)
    item_one = scale_i[...] * rs_end(0)
    isum[...] = i0[...] + item_one
    push_items(1, item_one)
    user_one = scale_u[...] * to_users(fetched(1))
    send_terms(2, to_columns((scale_u[...] * user_one).astype(BF16)))
    ufin[...] = u0[...] + user_one
    build_picks(1)

    rs_start(1, 2)
    send_picks(3, 1)
    item_final = (isum[...] + scale_i[...] * rs_end(1)) / 3.0
    tables[2, pl.ds(0, 128), :] = item_final.astype(BF16)
    ag_start(2)
    build_picks(2)
    send_picks(4, 2)
    build_picks(3)
    ufin[...] = (ufin[...] + scale_u[...] * to_users(fetched(3))) / 3.0

    final = fetched(4)
    exps = []
    for k in range(4):
        rows = jnp.dot(final, oh[k], preferred_element_type=F32)
        picked[k] = rows
        exps.append(jnp.exp(jnp.sum(ufin[...] * rows, axis=0, keepdims=True)))
    total = exps[0] + exps[1] + exps[2] + exps[3]
    slopes = [e / total - (1.0 if k == 0 else 0.0) for k, e in enumerate(exps)]
    spread = jnp.zeros((256, 1024), F32)
    for k in range(4):
        exact = slopes[k] * ufin[...]
        high = exact.astype(BF16)
        low = (exact - high.astype(F32)).astype(BF16)
        spread = spread + lax.dot_general(
            jnp.concatenate([high, low], axis=0), oh[k], NT, preferred_element_type=F32
        )
    send_terms(5, spread[:128] + spread[128:])
    grad = slopes[0] * picked[0]
    for k in range(1, 4):
        grad = grad + slopes[k] * picked[k]
    grad = grad / 3.0
    gu[...] = grad
    down_terms = to_columns((scale_u[...] * grad).astype(BF16))

    rs_start(2, 5)
    send_terms(6, down_terms)
    item_down = rs_end(2) / 3.0
    push_items(3, item_down)
    gi[...] = item_down
    send_picks(7, 3)
    rs_start(3, 6)
    first_item = scale_i[...] * rs_end(3)
    push_items(4, first_item)
    gi[...] = gi[...] + first_item
    first_user = scale_u[...] * to_users(fetched(7))
    send_terms(8, to_columns((scale_u[...] * first_user).astype(BF16)))
    gu[...] = gu[...] + first_user
    rs_start(4, 8)
    send_picks(9, 4)
    out_s[...] = (gi[...] + scale_i[...] * rs_end(4)).astype(BF16)
    own_o = pltpu.make_async_copy(
        out_s.at[pl.ds(pl.multiple_of(near * 16, 16), 16)], out_r.at[me], o_sem.at[1]
    )
    own_o.start()

    @pl.loop(0, PEERS - 1)
    def _(k):
        to, _, n_to = peer(k)
        rows = pl.ds(pl.multiple_of(n_to * 16, 16), 16)
        remote(out_s.at[rows], out_r.at[me], o_sem.at[0], o_sem.at[1], to)

    gu_out[...] = (gu[...] + scale_u[...] * to_users(fetched(9))).T
    await_bytes(out_r, o_sem.at[1])

    @pl.loop(0, PEERS)
    def _(p):
        rows = out_r[p].astype(F32)
        for e in range(2):
            wide[pl.ds(p * 2 + e, 16, stride=128), :] = rows[:, e * 128 : e * 128 + 128]

    @pl.loop(0, 16)
    def _(blk):
        rows = pl.ds(pl.multiple_of(blk * 128, 128), 128)
        gi_out[rows, :] = wide[rows, :].T

    await_bytes(xs.at[pl.ds(0, NEAR - 1)], x_sem.at[0])
    await_bytes(dr.at[pl.ds(0, NEAR - 1)], d_sem.at[0])
    await_bytes(cr.at[pl.ds(0, PEERS - 1)], c_sem.at[0])
    await_bytes(out_r.at[pl.ds(0, PEERS - 1)], o_sem.at[0])
    for n in range(10):
        await_bytes(zs.at[n, pl.ds(0, PEERS - 1)], z_send.at[n])
    for n in range(5):
        await_bytes(tables.at[n, pl.ds(128, 384)], ag_send.at[n])
        await_bytes(rb[n], rs_send.at[n])


def on_device(
    user_emb, item_emb, user_deg, item_deg, blk_rows, blk_slot, fetch_cols, blk_mask, samples
):
    smem = pl.BlockSpec(memory_space=pltpu.SMEM)
    vmem = pl.BlockSpec(memory_space=pltpu.VMEM)
    mat = pl.pallas_call(
        place_kernel,
        out_shape=jax.ShapeDtypeStruct((1024, 1024), BF16),
        in_specs=[smem, smem, vmem],
        out_specs=vmem,
        compiler_params=pltpu.CompilerParams(vmem_limit_bytes=16 * 2**20),
        name="place_blocks",
    )(blk_rows, blk_slot, blk_mask)
    dma = pltpu.SemaphoreType.DMA
    state = pltpu.VMEM((128, 256), F32)
    users = pltpu.VMEM((128, 1024), F32)
    return pl.pallas_call(
        main_kernel,
        out_shape=(
            jax.ShapeDtypeStruct((1024, 128), F32),
            jax.ShapeDtypeStruct((2048, 128), F32),
        ),
        in_specs=[smem] + [vmem] * 6,
        out_specs=(vmem, vmem),
        scratch_shapes=[
            users, pltpu.VMEM((1, 1024), F32), state, state, users, users, state, state,
            pltpu.VMEM((4, 1024, 1024), BF16), pltpu.VMEM((4, 128, 1024), F32),
            pltpu.VMEM((512, 512), BF16), pltpu.VMEM((512, 512), BF16),
            pltpu.VMEM((5, 512, 256), BF16),
            pltpu.VMEM((10, PEERS, 16, 128), BF16), pltpu.VMEM((10, PEERS, 16, 128), BF16),
            pltpu.VMEM((1, 128), I32), pltpu.VMEM((PEERS, 1, 128), I32),
            pltpu.VMEM((NEAR, 16, 256), BF16), pltpu.VMEM((NEAR, 16, 256), BF16),
            pltpu.VMEM((16, 128), F32), pltpu.VMEM((NEAR, 16, 128), F32),
            pltpu.VMEM((1024, 128), F32), pltpu.VMEM((2048, 128), F32),
            pltpu.VMEM((2, 128, 256), F32),
            *[pltpu.VMEM((3, 128, 256), t) for t in RS_TYPES],
            *[pltpu.VMEM((3, 128, 256), t) for t in RS_TYPES],
            pltpu.VMEM((128, 256), BF16), pltpu.VMEM((PEERS, 16, 256), BF16),
            dma((10,)), dma((10,)), dma((2,)), dma((2,)), dma((2,)),
            dma((5,)), dma((5,)), dma((5,)), dma((5,)), dma((2,)),
        ],
        compiler_params=pltpu.CompilerParams(
            collective_id=0, has_side_effects=True, vmem_limit_bytes=56 * 2**20
        ),
        name="gcn",
    )(
        fetch_cols, user_emb, item_emb, user_deg.reshape(1, -1), item_deg.reshape(16, 128),
        samples.T, mat,
    )


def solution(mesh):
    both = ("ugrp", "item")
    return jax.shard_map(
        on_device,
        mesh=mesh,
        in_specs=(
            P(both, None), P("item", None), P(both), P("item"), P(both), P(both), P(both),
            P(both, None, None), P(both, None),
        ),
        out_specs=(P(both, None), P("item", None)),
        check_vma=False,
    )
```

```python
import jax
import jax.numpy as jnp
from jax import lax
from jax.experimental import pallas as pl
from jax.experimental.pallas import tpu as pltpu
from jax.sharding import PartitionSpec as P

F32, BF16, I32 = jnp.float32, jnp.bfloat16, jnp.int32
MESH = pl.DeviceIdType.MESH
NT = (((1,), (1,)), ((), ()))
NZ, PEERS, NEAR = 8, 64, 8
RS_TYPES = (BF16, BF16, F32, BF16, BF16)


def finish_kernel(gu_t, gi_t, gu_out, gi_out):
    gu_out[...] = gu_t[...].T
    for blk in range(4):
        gi_out[pl.ds(blk * 128, 128), :] = gi_t[pl.ds(blk * 128, 128), :].T


def main_kernel(
    cols, uemb, iemb, udeg, ideg, picks, rows_in, slots_in, mask_in,
    gu_out, gi_out,
    u0, scale_u, i0, scale_i, ufin, gu, gi, isum,
    oh, picked, sel, selt, tables, zs, zr, cs, cr, xs, xr, ds, dr, relay, mask, wide_mat, mat,
    pf, sb0, sb1, sb2, sb3, sb4, rb0, rb1, rb2, rb3, rb4, out_s, out_r,
    z_send, z_recv, c_sem, x_sem, d_sem, ag_send, ag_recv, rs_send, rs_recv, o_send, o_recv, m_sem,
):
    sb, rb = (sb0, sb1, sb2, sb3, sb4), (rb0, rb1, rb2, rb3, rb4)
    z, j = lax.axis_index("ugrp"), lax.axis_index("item")
    c = j % 2
    x, y = (j // 2) % 4, j // 8
    nc = 1 - c
    p, r = x * nc + y * c, y * nc + x * c
    near = p * 2 + c
    me = z * NEAR + near

    def device(x_to, y_to, c_to):
        return (y_to * 4 + x_to) * 2 + c_to

    def along(d):
        r_to = (r + d) % 4
        return (z, device(p * nc + r_to * c, r_to * nc + p * c, c))

    def offset(k):
        return (p + k // 2) % 4, (c + k % 2) % 2

    def plane(i):
        return (z + 4 + ((i + 1) // 2) * (1 - 2 * (i % 2))) % NZ

    def to_user(k):
        p_to, c_to = offset(k)
        return device(p_to * nc + x * c, y * nc + p_to * c, c_to), p_to * 2 + c_to

    def to_holder(k):
        p_to, c_to = offset(k)
        j_to = device(p_to * (1 - c_to) + x * c_to, y * (1 - c_to) + p_to * c_to, c_to)
        return j_to, p_to * 2 + c_to, (x * (1 - c_to) + y * c_to) * 2 + c

    def remote(src, dst, send, recv, to):
        pltpu.make_async_remote_copy(
            src_ref=src, dst_ref=dst, send_sem=send, recv_sem=recv, device_id=to, device_id_type=MESH
        ).start()

    def await_bytes(ref, sem):
        pltpu.make_async_copy(ref, ref, sem).wait()

    mask_copy = pltpu.make_async_copy(mask_in, mask, m_sem)
    mask_copy.start()
    barrier = pltpu.get_barrier_semaphore()

    def greet(to):
        pl.semaphore_signal(barrier, inc=1, device_id=to, device_id_type=MESH)

    for d in (1, 2, 3):
        greet(along(d))

    @pl.loop(0, PEERS - 1)
    def _(k):
        greet((plane(k // NEAR), to_user(NEAR - 1 - k % NEAR)[0]))

    @pl.loop(0, 3 * NZ)
    def _(k):
        d = k // NZ + 1
        greet((k % NZ, device((x + d * c) % 4, (y + d * nc) % 4, nc)))

    def own_start(n):
        own = pltpu.make_async_copy(zs.at[n, me], zr.at[n, me], z_recv.at[n])
        own.start()

    def to_users_start(n):
        own_start(n)

        @pl.loop(0, PEERS - 1)
        def _(k):
            z_to = plane(k // NEAR)
            j_to, slot = to_user(NEAR - 1 - k % NEAR)
            remote(
                zs.at[n, z_to * NEAR + slot], zr.at[n, me], z_send.at[n], z_recv.at[n], (z_to, j_to)
            )

    def to_holders_start(n):
        own_start(n)

        @pl.loop(0, PEERS - 1)
        def _(k):
            z_to = plane(k // NEAR)
            j_to, slot, there = to_holder(NEAR - 1 - k % NEAR)
            remote(
                zs.at[n, z_to * NEAR + slot], zr.at[n, z * NEAR + there],
                z_send.at[n], z_recv.at[n], (z_to, j_to),
            )

    def z_wait(n):
        await_bytes(zr.at[n], z_recv.at[n])

    def ag_start(n):
        for d in (2, 1, 3):
            remote(
                tables.at[n, pl.ds(0, 128)], tables.at[n, pl.ds((4 - d) * 128, 128)],
                ag_send.at[n], ag_recv.at[n], along(d),
            )

    def ag_wait(n):
        await_bytes(tables.at[n, pl.ds(128, 384)], ag_recv.at[n])

    def rs_start(n, zn):
        z_wait(zn)
        got = zr[zn].astype(F32)
        terms = jnp.concatenate(
            [got[:, :8].reshape(512, 128), got[:, 8:].reshape(512, 128)], axis=1
        ).astype(BF16)
        for d in (2, 1, 3, 0):
            part = jnp.dot(selt[pl.ds(d * 128, 128), :], terms, preferred_element_type=F32)
            if d:
                sb[n][d - 1] = part.astype(sb[n].dtype)
                remote(sb[n].at[d - 1], rb[n].at[d - 1], rs_send.at[n], rs_recv.at[n], along(d))
            else:
                pf[n % 2] = part

    def rs_end(n):
        await_bytes(rb[n], rs_recv.at[n])
        return pf[n % 2] + rb[n][0].astype(F32) + rb[n][1].astype(F32) + rb[n][2].astype(F32)

    def send_terms(zn, terms):
        for f in range(8):
            relay[pl.ds(f, 128, stride=8), :] = terms[:, f * 128 : f * 128 + 128]
        zs[zn] = relay[...].reshape(PEERS, 16, 128).astype(BF16)
        to_holders_start(zn)

    def send_picks(zn, n):
        ag_wait(n)
        found = jnp.dot(sel[...], tables[n], preferred_element_type=F32)
        zs[zn] = jnp.concatenate(
            [found[:, :128].reshape(PEERS, 8, 128), found[:, 128:].reshape(PEERS, 8, 128)], axis=1
        ).astype(BF16)
        to_users_start(zn)

    def fetched(zn):
        z_wait(zn)
        relay[...] = zr[zn].astype(F32).reshape(1024, 128)
        return jnp.concatenate(
            [relay[pl.ds(f, 128, stride=8), :] for f in range(8)], axis=1
        ).astype(BF16)

    def to_users(rows):
        return lax.dot_general(rows, mat[...], NT, preferred_element_type=F32)

    def to_columns(rows):
        return jnp.dot(rows, mat[...], preferred_element_type=F32)

    def push_items(n, rows):
        tables[n, pl.ds(0, 128), :] = (scale_i[...] * rows).astype(BF16)
        ag_start(n)

    def build_picks(k):
        line = picks[pl.ds(k, 1), :]

        @pl.loop(0, 8)
        def _(r):
            at_row = pl.multiple_of(r * 128, 128)
            number = lax.broadcasted_iota(I32, (128, 1024), 0) + at_row
            oh[k, pl.ds(at_row, 128), :] = jnp.where(number == line, 1.0, 0.0).astype(BF16)

    lane_row = lax.broadcasted_iota(I32, (1, 128), 1) & 7
    want = jnp.zeros((1, 128), I32)
    for f in range(8):
        want = jnp.where(lane_row == f, cols[f], want)
    cs[...] = want
    cr[me] = want
    lane = lax.broadcasted_iota(I32, (16, 128), 1)
    row = lax.broadcasted_iota(I32, (16, 128), 0)
    some = lax.dot_general(
        jnp.where(lane == z * 16 + row, 1.0, 0.0).astype(BF16), iemb[...], NT,
        preferred_element_type=F32,
    )
    for blk in range(16):
        relay[pl.ds(blk * 16, 16), :] = some[:, blk * 128 : blk * 128 + 128]
    for q in range(NEAR):
        xs[q] = jnp.concatenate(
            [relay[pl.ds(q * 2 + e, 16, stride=16), :] for e in range(2)], axis=1
        ).astype(BF16)
    ds[...] = lax.rsqrt(ideg[...].astype(F32))

    pl.semaphore_wait(barrier, 3 + PEERS - 1 + 3 * NZ)

    own_x = pltpu.make_async_copy(xs.at[near], xr.at[near], x_sem.at[1])
    own_x.start()
    own_d = pltpu.make_async_copy(ds, dr.at[near], d_sem.at[1])
    own_d.start()

    @pl.loop(1, NEAR)
    def _(k):
        j_to, slot, there = to_holder(k)
        remote(xs.at[slot], xr.at[there], x_sem.at[0], x_sem.at[1], (z, j_to))
        remote(ds, dr.at[there], d_sem.at[0], d_sem.at[1], (z, j_to))

    @pl.loop(0, PEERS - 1)
    def _(k):
        z_to = plane(k // NEAR)
        j_to, _, there = to_holder(NEAR - 1 - k % NEAR)
        remote(cs, cr.at[z * NEAR + there], c_sem.at[0], c_sem.at[1], (z_to, j_to))

    eye = jnp.where(
        lax.broadcasted_iota(I32, (128, 128), 0) == lax.broadcasted_iota(I32, (128, 128), 1), 1.0, 0.0
    ).astype(BF16)
    user_rows = lax.dot_general(eye, uemb[...], NT, preferred_element_type=F32)
    u0[...] = user_rows
    scale_u[...] = lax.rsqrt(udeg[...].astype(F32))
    await_bytes(xr, x_sem.at[1])
    await_bytes(dr, d_sem.at[1])
    i0[...] = xr[...].astype(F32).reshape(128, 256)
    one_scale = dr[...].reshape(128, 128)
    scale_i[...] = jnp.concatenate([one_scale, one_scale], axis=1)
    push_items(0, i0[...])

    cell = slots_in[...] * 8 + rows_in[...]
    where = jnp.where(lax.broadcasted_iota(I32, (64, 32), 0) == cell, 1.0, 0.0).astype(BF16)
    mask_copy.wait()
    lines = mask.reshape(32 * 128, 128)

    @pl.loop(0, 16)
    def _(group):
        for step in range(8):
            i = group * 8 + step
            line = lines[pl.ds(i, 32, stride=128), :].astype(F32).astype(BF16)
            sums = jnp.dot(where, line, preferred_element_type=F32)
            wide_mat[pl.ds(i, 64, stride=128), :] = sums

    for f in range(8):
        mat[:, f * 128 : f * 128 + 128] = wide_mat[pl.ds(f * 1024, 1024), :].astype(BF16)

    await_bytes(cr.at[pl.ds(0, PEERS - 1)], c_sem.at[1])
    col = cr[...]
    x_of = lax.shift_right_logical(col, jnp.full_like(col, 5)) & 3
    y_of = lax.shift_right_logical(col, jnp.full_like(col, 7))
    r_of, p_of = y_of * nc + x_of * c, x_of * nc + y_of * c
    place = (((r_of - r + 4) & 3) * 128 + p_of * 32 + (col & 31)).astype(F32)
    mine = (lax.broadcasted_iota(I32, (8, 128), 1) & 7) == lax.broadcasted_iota(I32, (8, 128), 0)
    spot = jnp.sum(
        jnp.where(mine[None], jnp.broadcast_to(place, (PEERS, 8, 128)), 0.0), axis=2, keepdims=True
    ) * (1.0 / 16.0)
    spot = jnp.broadcast_to(spot, (PEERS, 8, 128)).reshape(512, 128)
    for q in range(4):
        sel[:, q * 128 : q * 128 + 128] = jnp.where(
            spot == (lax.broadcasted_iota(I32, (512, 128), 1) + q * 128).astype(F32), 1.0, 0.0
        ).astype(BF16)
        turned = spot[q * 128 : q * 128 + 128].T
        for m in range(4):
            selt[m * 128 : m * 128 + 128, q * 128 : q * 128 + 128] = jnp.where(
                turned == (lax.broadcasted_iota(I32, (128, 128), 0) + m * 128).astype(F32), 1.0, 0.0
            ).astype(BF16)

    send_picks(1, 0)
    send_terms(0, to_columns((scale_u[...] * u0[...]).astype(BF16)))
    build_picks(0)
    user_one = scale_u[...] * to_users(fetched(1))
    send_terms(2, to_columns((scale_u[...] * user_one).astype(BF16)))
    rs_start(0, 0)
    ufin[...] = u0[...] + user_one
    build_picks(1)
    item_one = scale_i[...] * rs_end(0)
    isum[...] = i0[...] + item_one
    push_items(1, item_one)

    rs_start(1, 2)
    send_picks(3, 1)
    item_final = (isum[...] + scale_i[...] * rs_end(1)) / 3.0
    tables[2, pl.ds(0, 128), :] = item_final.astype(BF16)
    ag_start(2)
    build_picks(2)
    send_picks(4, 2)
    build_picks(3)
    ufin[...] = (ufin[...] + scale_u[...] * to_users(fetched(3))) / 3.0

    final = fetched(4)
    exps = []
    for k in range(4):
        rows = jnp.dot(final, oh[k], preferred_element_type=F32)
        picked[k] = rows
        exps.append(jnp.exp(jnp.sum(ufin[...] * rows, axis=0, keepdims=True)))
    total = exps[0] + exps[1] + exps[2] + exps[3]
    slopes = [e / total - (1.0 if k == 0 else 0.0) for k, e in enumerate(exps)]
    spread = jnp.zeros((256, 1024), F32)
    for k in range(4):
        exact = slopes[k] * ufin[...]
        high = exact.astype(BF16)
        low = (exact - high.astype(F32)).astype(BF16)
        spread = spread + lax.dot_general(
            jnp.concatenate([high, low], axis=0), oh[k], NT, preferred_element_type=F32
        )
    send_terms(5, spread[:128] + spread[128:])
    grad = slopes[0] * picked[0]
    for k in range(1, 4):
        grad = grad + slopes[k] * picked[k]
    grad = grad / 3.0
    gu[...] = grad
    down_terms = to_columns((scale_u[...] * grad).astype(BF16))

    rs_start(2, 5)
    send_terms(6, down_terms)
    item_down = rs_end(2) / 3.0
    push_items(3, item_down)
    gi[...] = item_down
    send_picks(7, 3)
    rs_start(3, 6)
    first_item = scale_i[...] * rs_end(3)
    push_items(4, first_item)
    gi[...] = gi[...] + first_item
    first_user = scale_u[...] * to_users(fetched(7))
    send_terms(8, to_columns((scale_u[...] * first_user).astype(BF16)))
    gu[...] = gu[...] + first_user
    rs_start(4, 8)
    send_picks(9, 4)
    out_s[...] = (gi[...] + scale_i[...] * rs_end(4)).astype(BF16)
    own_o = pltpu.make_async_copy(
        out_s.at[pl.ds(pl.multiple_of(near * 16, 16), 16)], out_r.at[me], o_recv.at[2]
    )
    own_o.start()

    def out_step(z_to, k, arrival):
        j_to, slot = to_user(k)
        rows = pl.ds(pl.multiple_of(slot * 16, 16), 16)
        remote(out_s.at[rows], out_r.at[me], o_send.at[0], o_recv.at[arrival], (z_to, j_to))

    for d, arrival in ((2, 0), (6, 1), (1, 2), (7, 2)):

        @pl.loop(0, NEAR)
        def _(k):
            out_step((z + d) % NZ, k, arrival)

    @pl.loop(1, NEAR)
    def _(k):
        out_step(z, k, 2)

    def hand_on(d_from, first, count, d_to, sent, arrival):
        part = out_r.at[pl.ds((z + d_from) % NZ * NEAR + first, count)]
        remote(part, part, o_send.at[sent], o_recv.at[arrival], ((z + d_to) % NZ, j))

    await_bytes(out_r.at[pl.ds(0, 8)], o_recv.at[0])
    hand_on(6, 0, 8, 1, 1, 3)
    hand_on(6, 0, 4, 2, 2, 4)
    await_bytes(out_r.at[pl.ds(0, 8)], o_recv.at[1])
    hand_on(2, 0, 8, 7, 3, 5)
    hand_on(2, 4, 4, 6, 4, 6)
    gu_out[...] = gu[...] + scale_u[...] * to_users(fetched(9))
    await_bytes(out_r.at[pl.ds(0, 24)], o_recv.at[2])
    for arrival, count in ((3, 8), (5, 8), (4, 4), (6, 4)):
        await_bytes(out_r.at[pl.ds(0, count)], o_recv.at[arrival])

    @pl.loop(0, PEERS)
    def _(s):
        rows = out_r[s].astype(F32)
        for e in range(2):
            gi_out[pl.ds(s * 2 + e, 16, stride=128), :] = rows[:, e * 128 : e * 128 + 128]

    await_bytes(xs.at[pl.ds(0, NEAR - 1)], x_sem.at[0])
    await_bytes(dr.at[pl.ds(0, NEAR - 1)], d_sem.at[0])
    await_bytes(cr.at[pl.ds(0, PEERS - 1)], c_sem.at[0])
    await_bytes(out_r.at[pl.ds(0, 39)], o_send.at[0])
    for sent, count in ((1, 8), (2, 4), (3, 8), (4, 4)):
        await_bytes(out_r.at[pl.ds(0, count)], o_send.at[sent])
    for n in range(10):
        await_bytes(zs.at[n, pl.ds(0, PEERS - 1)], z_send.at[n])
    for n in range(5):
        await_bytes(tables.at[n, pl.ds(128, 384)], ag_send.at[n])
        await_bytes(rb[n], rs_send.at[n])


def on_device(
    user_emb, item_emb, user_deg, item_deg, blk_rows, blk_slot, fetch_cols, blk_mask, samples
):
    smem = pl.BlockSpec(memory_space=pltpu.SMEM)
    vmem = pl.BlockSpec(memory_space=pltpu.VMEM)
    dma = pltpu.SemaphoreType.DMA
    state = pltpu.VMEM((128, 256), F32)
    users = pltpu.VMEM((128, 1024), F32)
    gu_t, gi_t = pl.pallas_call(
        main_kernel,
        out_shape=(
            jax.ShapeDtypeStruct((128, 1024), F32),
            jax.ShapeDtypeStruct((2048, 128), F32),
        ),
        in_specs=[smem] + [vmem] * 7 + [pl.BlockSpec(memory_space=pl.ANY)],
        out_specs=(vmem, vmem),
        scratch_shapes=[
            users, pltpu.VMEM((1, 1024), F32), state, state, users, users, state, state,
            pltpu.VMEM((4, 1024, 1024), BF16), pltpu.VMEM((4, 128, 1024), F32),
            pltpu.VMEM((512, 512), BF16), pltpu.VMEM((512, 512), BF16),
            pltpu.VMEM((5, 512, 256), BF16),
            pltpu.VMEM((10, PEERS, 16, 128), BF16), pltpu.VMEM((10, PEERS, 16, 128), BF16),
            pltpu.VMEM((1, 128), I32), pltpu.VMEM((PEERS, 1, 128), I32),
            pltpu.VMEM((NEAR, 16, 256), BF16), pltpu.VMEM((NEAR, 16, 256), BF16),
            pltpu.VMEM((16, 128), F32), pltpu.VMEM((NEAR, 16, 128), F32),
            pltpu.VMEM((1024, 128), F32), pltpu.VMEM((32, 128, 128), I32),
            pltpu.VMEM((8192, 128), F32), pltpu.VMEM((1024, 1024), BF16),
            pltpu.VMEM((2, 128, 256), F32),
            *[pltpu.VMEM((3, 128, 256), t) for t in RS_TYPES],
            *[pltpu.VMEM((3, 128, 256), t) for t in RS_TYPES],
            pltpu.VMEM((128, 256), BF16), pltpu.VMEM((PEERS, 16, 256), BF16),
            dma((10,)), dma((10,)), dma((2,)), dma((2,)), dma((2,)),
            dma((5,)), dma((5,)), dma((5,)), dma((5,)), dma((5,)), dma((7,)), dma,
        ],
        compiler_params=pltpu.CompilerParams(
            collective_id=0, has_side_effects=True, vmem_limit_bytes=56 * 2**20
        ),
        name="gcn",
    )(
        fetch_cols, user_emb, item_emb, user_deg.reshape(1, -1), item_deg.reshape(16, 128),
        samples.T, blk_rows.reshape(1, -1), blk_slot.reshape(1, -1), blk_mask,
    )
    return pl.pallas_call(
        finish_kernel,
        grid=(4,),
        out_shape=(
            jax.ShapeDtypeStruct((1024, 128), F32),
            jax.ShapeDtypeStruct((2048, 128), F32),
        ),
        in_specs=[
            pl.BlockSpec((128, 256), lambda i: (0, i)),
            pl.BlockSpec((512, 128), lambda i: (i, 0)),
        ],
        out_specs=(
            pl.BlockSpec((256, 128), lambda i: (i, 0)),
            pl.BlockSpec((512, 128), lambda i: (i, 0)),
        ),
        compiler_params=pltpu.CompilerParams(vmem_limit_bytes=8 * 2**20),
        name="finish",
    )(gu_t, gi_t)


def solution(mesh):
    both = ("ugrp", "item")
    return jax.shard_map(
        on_device,
        mesh=mesh,
        in_specs=(
            P(both, None), P("item", None), P(both), P("item"), P(both), P(both), P(both),
            P(both, None, None), P(both, None),
        ),
        out_specs=(P(both, None), P("item", None)),
        check_vma=False,
    )
```

```python
import jax
import jax.numpy as jnp
from jax import lax
from jax.experimental import pallas as pl
from jax.experimental.pallas import tpu as pltpu
from jax.sharding import PartitionSpec as P

F32, BF16, I32 = jnp.float32, jnp.bfloat16, jnp.int32
MESH = pl.DeviceIdType.MESH
NT = (((1,), (1,)), ((), ()))
NZ, PEERS, NEAR = 8, 64, 8
RS_TYPES = (BF16, BF16, F32, BF16, BF16)


def finish_kernel(gu_t, gi_t, gu_out, gi_out):
    gu_out[...] = gu_t[...].T
    for blk in range(4):
        gi_out[pl.ds(blk * 128, 128), :] = gi_t[pl.ds(blk * 128, 128), :].T


def main_kernel(
    cols_in, uemb_in, iemb_in, udeg_in, ideg_in, picks_in, rows_in, slots_in, mask_in,
    gu_out, gi_out,
    u0, scale_u, i0, scale_i, ufin, gu, gi, isum,
    oh, picked, sel, selt, tables, zs, zr, cs, cr, xs, xr, ds, dr, relay, wide_mat, mat,
    cols, uemb, iemb, udeg, ideg, picks, rows, slots, mask,
    pf, sb0, sb1, sb2, sb3, sb4, rb0, rb1, rb2, rb3, rb4, out_s, out_r,
    z_send, z_recv, c_sem, x_sem, d_sem, ag_send, ag_recv, rs_send, rs_recv, o_send, o_recv, m_sem,
):
    sb, rb = (sb0, sb1, sb2, sb3, sb4), (rb0, rb1, rb2, rb3, rb4)
    z, j = lax.axis_index("ugrp"), lax.axis_index("item")
    c = j % 2
    x, y = (j // 2) % 4, j // 8
    nc = 1 - c
    p, r = x * nc + y * c, y * nc + x * c
    near = p * 2 + c
    me = z * NEAR + near

    def device(x_to, y_to, c_to):
        return (y_to * 4 + x_to) * 2 + c_to

    def along(d):
        r_to = (r + d) % 4
        return (z, device(p * nc + r_to * c, r_to * nc + p * c, c))

    def offset(k):
        return (p + k // 2) % 4, (c + k % 2) % 2

    def plane(i):
        return (z + 4 + ((i + 1) // 2) * (1 - 2 * (i % 2))) % NZ

    def to_user(k):
        p_to, c_to = offset(k)
        return device(p_to * nc + x * c, y * nc + p_to * c, c_to), p_to * 2 + c_to

    def to_holder(k):
        p_to, c_to = offset(k)
        j_to = device(p_to * (1 - c_to) + x * c_to, y * (1 - c_to) + p_to * c_to, c_to)
        return j_to, p_to * 2 + c_to, (x * (1 - c_to) + y * c_to) * 2 + c

    def remote(src, dst, send, recv, to):
        pltpu.make_async_remote_copy(
            src_ref=src, dst_ref=dst, send_sem=send, recv_sem=recv, device_id=to, device_id_type=MESH
        ).start()

    def await_bytes(ref, sem):
        pltpu.make_async_copy(ref, ref, sem).wait()

    brought = {}
    for n, (name, src, dst) in enumerate((
        ("iemb", iemb_in, iemb), ("ideg", ideg_in, ideg), ("cols", cols_in, cols),
        ("uemb", uemb_in, uemb), ("udeg", udeg_in, udeg), ("rows", rows_in, rows),
        ("slots", slots_in, slots), ("mask", mask_in, mask), ("picks", picks_in, picks),
    )):
        brought[name] = pltpu.make_async_copy(src, dst, m_sem.at[n])
        brought[name].start()
    barrier = pltpu.get_barrier_semaphore()

    def greet(to):
        pl.semaphore_signal(barrier, inc=1, device_id=to, device_id_type=MESH)

    for d in (1, 2, 3):
        greet(along(d))

    @pl.loop(0, PEERS - 1)
    def _(k):
        greet((plane(k // NEAR), to_user(NEAR - 1 - k % NEAR)[0]))

    @pl.loop(0, 3 * NZ)
    def _(k):
        d = k // NZ + 1
        greet((k % NZ, device((x + d * c) % 4, (y + d * nc) % 4, nc)))

    def own_start(n):
        own = pltpu.make_async_copy(zs.at[n, me], zr.at[n, me], z_recv.at[n])
        own.start()

    def to_users_start(n):
        own_start(n)

        @pl.loop(0, PEERS - 1)
        def _(k):
            z_to = plane(k // NEAR)
            j_to, slot = to_user(NEAR - 1 - k % NEAR)
            remote(
                zs.at[n, z_to * NEAR + slot], zr.at[n, me], z_send.at[n], z_recv.at[n], (z_to, j_to)
            )

    def to_holders_start(n):
        own_start(n)

        @pl.loop(0, PEERS - 1)
        def _(k):
            z_to = plane(k // NEAR)
            j_to, slot, there = to_holder(NEAR - 1 - k % NEAR)
            remote(
                zs.at[n, z_to * NEAR + slot], zr.at[n, z * NEAR + there],
                z_send.at[n], z_recv.at[n], (z_to, j_to),
            )

    def z_wait(n):
        await_bytes(zr.at[n], z_recv.at[n])

    def ag_start(n):
        for d in (2, 1, 3):
            remote(
                tables.at[n, pl.ds(0, 128)], tables.at[n, pl.ds((4 - d) * 128, 128)],
                ag_send.at[n], ag_recv.at[n], along(d),
            )

    def ag_wait(n):
        await_bytes(tables.at[n, pl.ds(128, 384)], ag_recv.at[n])

    def rs_start(n, zn):
        z_wait(zn)
        got = zr[zn].astype(F32)
        terms = jnp.concatenate(
            [got[:, :8].reshape(512, 128), got[:, 8:].reshape(512, 128)], axis=1
        ).astype(BF16)
        for d in (2, 1, 3, 0):
            part = jnp.dot(selt[pl.ds(d * 128, 128), :], terms, preferred_element_type=F32)
            if d:
                sb[n][d - 1] = part.astype(sb[n].dtype)
                remote(sb[n].at[d - 1], rb[n].at[d - 1], rs_send.at[n], rs_recv.at[n], along(d))
            else:
                pf[n % 2] = part

    def rs_end(n):
        await_bytes(rb[n], rs_recv.at[n])
        return pf[n % 2] + rb[n][0].astype(F32) + rb[n][1].astype(F32) + rb[n][2].astype(F32)

    def send_terms(zn, terms):
        for f in range(8):
            relay[pl.ds(f, 128, stride=8), :] = terms[:, f * 128 : f * 128 + 128]
        zs[zn] = relay[...].reshape(PEERS, 16, 128).astype(BF16)
        to_holders_start(zn)

    def send_picks(zn, n):
        ag_wait(n)
        found = jnp.dot(sel[...], tables[n], preferred_element_type=F32)
        zs[zn] = jnp.concatenate(
            [found[:, :128].reshape(PEERS, 8, 128), found[:, 128:].reshape(PEERS, 8, 128)], axis=1
        ).astype(BF16)
        to_users_start(zn)

    def fetched(zn):
        z_wait(zn)
        relay[...] = zr[zn].astype(F32).reshape(1024, 128)
        return jnp.concatenate(
            [relay[pl.ds(f, 128, stride=8), :] for f in range(8)], axis=1
        ).astype(BF16)

    def to_users(rows):
        return lax.dot_general(rows, mat[...], NT, preferred_element_type=F32)

    def to_columns(rows):
        return jnp.dot(rows, mat[...], preferred_element_type=F32)

    def push_items(n, rows):
        tables[n, pl.ds(0, 128), :] = (scale_i[...] * rows).astype(BF16)
        ag_start(n)

    def build_picks(k):
        line = picks[pl.ds(k, 1), :]

        @pl.loop(0, 8)
        def _(r):
            at_row = pl.multiple_of(r * 128, 128)
            number = lax.broadcasted_iota(I32, (128, 1024), 0) + at_row
            oh[k, pl.ds(at_row, 128), :] = jnp.where(number == line, 1.0, 0.0).astype(BF16)

    for name in ("cols", "iemb", "ideg"):
        brought[name].wait()
    lane_row = lax.broadcasted_iota(I32, (1, 128), 1) & 7
    want = jnp.zeros((1, 128), I32)
    for f in range(8):
        want = jnp.where(lane_row == f, cols[:, f : f + 1], want)
    cs[...] = want
    cr[me] = want
    lane = lax.broadcasted_iota(I32, (16, 128), 1)
    row = lax.broadcasted_iota(I32, (16, 128), 0)
    some = lax.dot_general(
        jnp.where(lane == z * 16 + row, 1.0, 0.0).astype(BF16), iemb[...], NT,
        preferred_element_type=F32,
    )
    for blk in range(16):
        relay[pl.ds(blk * 16, 16), :] = some[:, blk * 128 : blk * 128 + 128]
    for q in range(NEAR):
        xs[q] = jnp.concatenate(
            [relay[pl.ds(q * 2 + e, 16, stride=16), :] for e in range(2)], axis=1
        ).astype(BF16)
    ds[...] = lax.rsqrt(ideg[...].astype(F32))

    pl.semaphore_wait(barrier, 3 + PEERS - 1 + 3 * NZ)

    own_x = pltpu.make_async_copy(xs.at[near], xr.at[near], x_sem.at[1])
    own_x.start()
    own_d = pltpu.make_async_copy(ds, dr.at[near], d_sem.at[1])
    own_d.start()

    @pl.loop(1, NEAR)
    def _(k):
        j_to, slot, there = to_holder(k)
        remote(xs.at[slot], xr.at[there], x_sem.at[0], x_sem.at[1], (z, j_to))
        remote(ds, dr.at[there], d_sem.at[0], d_sem.at[1], (z, j_to))

    @pl.loop(0, PEERS - 1)
    def _(k):
        z_to = plane(k // NEAR)
        j_to, _, there = to_holder(NEAR - 1 - k % NEAR)
        remote(cs, cr.at[z * NEAR + there], c_sem.at[0], c_sem.at[1], (z_to, j_to))

    eye = jnp.where(
        lax.broadcasted_iota(I32, (128, 128), 0) == lax.broadcasted_iota(I32, (128, 128), 1), 1.0, 0.0
    ).astype(BF16)
    brought["uemb"].wait()
    brought["udeg"].wait()
    user_rows = lax.dot_general(eye, uemb[...], NT, preferred_element_type=F32)
    u0[...] = user_rows
    scale_u[...] = lax.rsqrt(udeg[...].astype(F32))
    await_bytes(xr, x_sem.at[1])
    await_bytes(dr, d_sem.at[1])
    i0[...] = xr[...].astype(F32).reshape(128, 256)
    one_scale = dr[...].reshape(128, 128)
    scale_i[...] = jnp.concatenate([one_scale, one_scale], axis=1)
    push_items(0, i0[...])

    await_bytes(cr.at[pl.ds(0, PEERS - 1)], c_sem.at[1])
    col = cr[...]
    x_of = lax.shift_right_logical(col, jnp.full_like(col, 5)) & 3
    y_of = lax.shift_right_logical(col, jnp.full_like(col, 7))
    r_of, p_of = y_of * nc + x_of * c, x_of * nc + y_of * c
    place = (((r_of - r + 4) & 3) * 128 + p_of * 32 + (col & 31)).astype(F32)
    mine = (lax.broadcasted_iota(I32, (8, 128), 1) & 7) == lax.broadcasted_iota(I32, (8, 128), 0)
    spot = jnp.sum(
        jnp.where(mine[None], jnp.broadcast_to(place, (PEERS, 8, 128)), 0.0), axis=2, keepdims=True
    ) * (1.0 / 16.0)
    spot = jnp.broadcast_to(spot, (PEERS, 8, 128)).reshape(512, 128)
    for q in range(4):
        sel[:, q * 128 : q * 128 + 128] = jnp.where(
            spot == (lax.broadcasted_iota(I32, (512, 128), 1) + q * 128).astype(F32), 1.0, 0.0
        ).astype(BF16)
        turned = spot[q * 128 : q * 128 + 128].T
        for m in range(4):
            selt[m * 128 : m * 128 + 128, q * 128 : q * 128 + 128] = jnp.where(
                turned == (lax.broadcasted_iota(I32, (128, 128), 0) + m * 128).astype(F32), 1.0, 0.0
            ).astype(BF16)

    send_picks(1, 0)

    for name in ("rows", "slots", "mask", "picks"):
        brought[name].wait()
    cell = slots[...] * 8 + rows[...]
    where = jnp.where(lax.broadcasted_iota(I32, (64, 32), 0) == cell, 1.0, 0.0).astype(BF16)
    lines = mask.reshape(32 * 128, 128)

    @pl.loop(0, 16)
    def _(group):
        for step in range(8):
            i = group * 8 + step
            line = lines[pl.ds(i, 32, stride=128), :].astype(F32).astype(BF16)
            sums = jnp.dot(where, line, preferred_element_type=F32)
            wide_mat[pl.ds(i, 64, stride=128), :] = sums

    for f in range(8):
        mat[:, f * 128 : f * 128 + 128] = wide_mat[pl.ds(f * 1024, 1024), :].astype(BF16)

    send_terms(0, to_columns((scale_u[...] * u0[...]).astype(BF16)))
    build_picks(0)
    user_one = scale_u[...] * to_users(fetched(1))
    send_terms(2, to_columns((scale_u[...] * user_one).astype(BF16)))
    rs_start(0, 0)
    ufin[...] = u0[...] + user_one
    build_picks(1)
    item_one = scale_i[...] * rs_end(0)
    isum[...] = i0[...] + item_one
    push_items(1, item_one)

    rs_start(1, 2)
    send_picks(3, 1)
    item_final = (isum[...] + scale_i[...] * rs_end(1)) / 3.0
    tables[2, pl.ds(0, 128), :] = item_final.astype(BF16)
    ag_start(2)
    build_picks(2)
    send_picks(4, 2)
    build_picks(3)
    ufin[...] = (ufin[...] + scale_u[...] * to_users(fetched(3))) / 3.0

    final = fetched(4)
    exps = []
    for k in range(4):
        rows = jnp.dot(final, oh[k], preferred_element_type=F32)
        picked[k] = rows
        exps.append(jnp.exp(jnp.sum(ufin[...] * rows, axis=0, keepdims=True)))
    total = exps[0] + exps[1] + exps[2] + exps[3]
    slopes = [e / total - (1.0 if k == 0 else 0.0) for k, e in enumerate(exps)]
    spread = jnp.zeros((256, 1024), F32)
    for k in range(4):
        exact = slopes[k] * ufin[...]
        high = exact.astype(BF16)
        low = (exact - high.astype(F32)).astype(BF16)
        spread = spread + lax.dot_general(
            jnp.concatenate([high, low], axis=0), oh[k], NT, preferred_element_type=F32
        )
    send_terms(5, spread[:128] + spread[128:])
    grad = slopes[0] * picked[0]
    for k in range(1, 4):
        grad = grad + slopes[k] * picked[k]
    grad = grad / 3.0
    gu[...] = grad
    down_terms = to_columns((scale_u[...] * grad).astype(BF16))

    rs_start(2, 5)
    send_terms(6, down_terms)
    item_down = rs_end(2) / 3.0
    push_items(3, item_down)
    gi[...] = item_down
    send_picks(7, 3)
    rs_start(3, 6)
    first_item = scale_i[...] * rs_end(3)
    push_items(4, first_item)
    gi[...] = gi[...] + first_item
    first_user = scale_u[...] * to_users(fetched(7))
    send_terms(8, to_columns((scale_u[...] * first_user).astype(BF16)))
    gu[...] = gu[...] + first_user
    rs_start(4, 8)
    send_picks(9, 4)
    out_s[...] = (gi[...] + scale_i[...] * rs_end(4)).astype(BF16)
    own_o = pltpu.make_async_copy(
        out_s.at[pl.ds(pl.multiple_of(near * 16, 16), 16)], out_r.at[me], o_recv.at[2]
    )
    own_o.start()

    def out_step(z_to, k, arrival):
        j_to, slot = to_user(k)
        rows = pl.ds(pl.multiple_of(slot * 16, 16), 16)
        remote(out_s.at[rows], out_r.at[me], o_send.at[0], o_recv.at[arrival], (z_to, j_to))

    for d, arrival in ((2, 0), (6, 1), (1, 2), (7, 2)):

        @pl.loop(0, NEAR)
        def _(k):
            out_step((z + d) % NZ, k, arrival)

    @pl.loop(1, NEAR)
    def _(k):
        out_step(z, k, 2)

    def hand_on(d_from, first, count, d_to, sent, arrival):
        part = out_r.at[pl.ds((z + d_from) % NZ * NEAR + first, count)]
        remote(part, part, o_send.at[sent], o_recv.at[arrival], ((z + d_to) % NZ, j))

    await_bytes(out_r.at[pl.ds(0, 8)], o_recv.at[0])
    hand_on(6, 0, 8, 1, 1, 3)
    hand_on(6, 0, 4, 2, 2, 4)
    await_bytes(out_r.at[pl.ds(0, 8)], o_recv.at[1])
    hand_on(2, 0, 8, 7, 3, 5)
    hand_on(2, 4, 4, 6, 4, 6)
    gu_out[...] = gu[...] + scale_u[...] * to_users(fetched(9))
    await_bytes(out_r.at[pl.ds(0, 24)], o_recv.at[2])
    for arrival, count in ((3, 8), (5, 8), (4, 4), (6, 4)):
        await_bytes(out_r.at[pl.ds(0, count)], o_recv.at[arrival])

    @pl.loop(0, PEERS)
    def _(s):
        rows = out_r[s].astype(F32)
        for e in range(2):
            gi_out[pl.ds(s * 2 + e, 16, stride=128), :] = rows[:, e * 128 : e * 128 + 128]

    await_bytes(xs.at[pl.ds(0, NEAR - 1)], x_sem.at[0])
    await_bytes(dr.at[pl.ds(0, NEAR - 1)], d_sem.at[0])
    await_bytes(cr.at[pl.ds(0, PEERS - 1)], c_sem.at[0])
    await_bytes(out_r.at[pl.ds(0, 39)], o_send.at[0])
    for sent, count in ((1, 8), (2, 4), (3, 8), (4, 4)):
        await_bytes(out_r.at[pl.ds(0, count)], o_send.at[sent])
    for n in range(10):
        await_bytes(zs.at[n, pl.ds(0, PEERS - 1)], z_send.at[n])
    for n in range(5):
        await_bytes(tables.at[n, pl.ds(128, 384)], ag_send.at[n])
        await_bytes(rb[n], rs_send.at[n])


def on_device(
    user_emb, item_emb, user_deg, item_deg, blk_rows, blk_slot, fetch_cols, blk_mask, samples
):
    hbm = pl.BlockSpec(memory_space=pltpu.HBM)
    vmem = pl.BlockSpec(memory_space=pltpu.VMEM)
    dma = pltpu.SemaphoreType.DMA
    state = pltpu.VMEM((128, 256), F32)
    users = pltpu.VMEM((128, 1024), F32)
    gu_t, gi_t = pl.pallas_call(
        main_kernel,
        out_shape=(
            jax.ShapeDtypeStruct((128, 1024), F32),
            jax.ShapeDtypeStruct((2048, 128), F32),
        ),
        in_specs=[hbm] * 9,
        out_specs=(vmem, vmem),
        scratch_shapes=[
            users, pltpu.VMEM((1, 1024), F32), state, state, users, users, state, state,
            pltpu.VMEM((4, 1024, 1024), BF16), pltpu.VMEM((4, 128, 1024), F32),
            pltpu.VMEM((512, 512), BF16), pltpu.VMEM((512, 512), BF16),
            pltpu.VMEM((5, 512, 256), BF16),
            pltpu.VMEM((10, PEERS, 16, 128), BF16), pltpu.VMEM((10, PEERS, 16, 128), BF16),
            pltpu.VMEM((1, 128), I32), pltpu.VMEM((PEERS, 1, 128), I32),
            pltpu.VMEM((NEAR, 16, 256), BF16), pltpu.VMEM((NEAR, 16, 256), BF16),
            pltpu.VMEM((16, 128), F32), pltpu.VMEM((NEAR, 16, 128), F32),
            pltpu.VMEM((1024, 128), F32),
            pltpu.VMEM((8192, 128), F32), pltpu.VMEM((1024, 1024), BF16),
            pltpu.VMEM((1, 8), I32), pltpu.VMEM((1024, 128), BF16), pltpu.VMEM((2048, 128), BF16),
            pltpu.VMEM((1, 1024), I32), pltpu.VMEM((16, 128), I32), pltpu.VMEM((4, 1024), I32),
            pltpu.VMEM((1, 32), I32), pltpu.VMEM((1, 32), I32), pltpu.VMEM((32, 128, 128), I32),
            pltpu.VMEM((2, 128, 256), F32),
            *[pltpu.VMEM((3, 128, 256), t) for t in RS_TYPES],
            *[pltpu.VMEM((3, 128, 256), t) for t in RS_TYPES],
            pltpu.VMEM((128, 256), BF16), pltpu.VMEM((PEERS, 16, 256), BF16),
            dma((10,)), dma((10,)), dma((2,)), dma((2,)), dma((2,)),
            dma((5,)), dma((5,)), dma((5,)), dma((5,)), dma((5,)), dma((7,)), dma((9,)),
        ],
        compiler_params=pltpu.CompilerParams(
            collective_id=0, has_side_effects=True, vmem_limit_bytes=56 * 2**20
        ),
        name="gcn",
    )(
        fetch_cols.reshape(1, -1), user_emb, item_emb, user_deg.reshape(1, -1), item_deg.reshape(16, 128),
        samples.T, blk_rows.reshape(1, -1), blk_slot.reshape(1, -1), blk_mask,
    )
    return pl.pallas_call(
        finish_kernel,
        grid=(4,),
        out_shape=(
            jax.ShapeDtypeStruct((1024, 128), F32),
            jax.ShapeDtypeStruct((2048, 128), F32),
        ),
        in_specs=[
            pl.BlockSpec((128, 256), lambda i: (0, i)),
            pl.BlockSpec((512, 128), lambda i: (i, 0)),
        ],
        out_specs=(
            pl.BlockSpec((256, 128), lambda i: (i, 0)),
            pl.BlockSpec((512, 128), lambda i: (i, 0)),
        ),
        compiler_params=pltpu.CompilerParams(vmem_limit_bytes=56 * 2**20),
        name="finish",
    )(gu_t, gi_t)


def solution(mesh):
    both = ("ugrp", "item")
    return jax.shard_map(
        on_device,
        mesh=mesh,
        in_specs=(
            P(both, None), P("item", None), P(both), P("item"), P(both), P(both), P(both),
            P(both, None, None), P(both, None),
        ),
        out_specs=(P(both, None), P("item", None)),
        check_vma=False,
    )
```

```python
import jax
import jax.numpy as jnp
from jax import lax
from jax.experimental import pallas as pl
from jax.experimental.pallas import tpu as pltpu
from jax.sharding import PartitionSpec as P

F32, BF16, I32 = jnp.float32, jnp.bfloat16, jnp.int32
MESH = pl.DeviceIdType.MESH
NT = (((1,), (1,)), ((), ()))
NZ, PEERS, NEAR = 8, 64, 8
RS_TYPES = (BF16, BF16, F32, BF16, BF16)


def finish_kernel(gu_t, gi_t, gu_out, gi_out):
    gu_out[...] = gu_t[...].T
    for blk in range(4):
        gi_out[pl.ds(blk * 128, 128), :] = gi_t[pl.ds(blk * 128, 128), :].T


def main_kernel(
    cols_in, uemb_in, iemb_in, udeg_in, ideg_in, picks_in, rows_in, slots_in, mask_in,
    gu_out, gi_out,
    u0, scale_u, i0, scale_i, ufin, gu, gi, isum,
    oh, picked, sel, selt, tables, zs, zr, cs, cr, xs, xr, ds, dr, relay, wide_mat, mat,
    cols, uemb, iemb, udeg, ideg, picks, rows, slots, mask,
    pf, sb0, sb1, sb2, sb3, sb4, rb0, rb1, rb2, rb3, rb4, out_s, out_r,
    z_send, z_recv, c_sem, x_sem, d_sem, ag_send, ag_recv, rs_send, rs_recv, o_send, o_recv, m_sem, entered,
):
    sb, rb = (sb0, sb1, sb2, sb3, sb4), (rb0, rb1, rb2, rb3, rb4)
    z, j = lax.axis_index("ugrp"), lax.axis_index("item")
    c = j % 2
    x, y = (j // 2) % 4, j // 8
    nc = 1 - c
    p, r = x * nc + y * c, y * nc + x * c
    near = p * 2 + c
    me = z * NEAR + near

    def device(x_to, y_to, c_to):
        return (y_to * 4 + x_to) * 2 + c_to

    def along(d):
        r_to = (r + d) % 4
        return (z, device(p * nc + r_to * c, r_to * nc + p * c, c))

    def offset(k):
        return (p + k // 2) % 4, (c + k % 2) % 2

    def plane(i):
        return (z + 4 + ((i + 1) // 2) * (1 - 2 * (i % 2))) % NZ

    def to_user(k):
        p_to, c_to = offset(k)
        return device(p_to * nc + x * c, y * nc + p_to * c, c_to), p_to * 2 + c_to

    def to_holder(k):
        p_to, c_to = offset(k)
        j_to = device(p_to * (1 - c_to) + x * c_to, y * (1 - c_to) + p_to * c_to, c_to)
        return j_to, p_to * 2 + c_to, (x * (1 - c_to) + y * c_to) * 2 + c

    def remote(src, dst, send, recv, to):
        pltpu.make_async_remote_copy(
            src_ref=src, dst_ref=dst, send_sem=send, recv_sem=recv, device_id=to, device_id_type=MESH
        ).start()

    def await_bytes(ref, sem):
        pltpu.make_async_copy(ref, ref, sem).wait()

    brought = {}
    for n, (name, src, dst) in enumerate((
        ("iemb", iemb_in, iemb), ("ideg", ideg_in, ideg), ("cols", cols_in, cols),
        ("uemb", uemb_in, uemb), ("udeg", udeg_in, udeg), ("rows", rows_in, rows),
        ("slots", slots_in, slots), ("mask", mask_in, mask), ("picks", picks_in, picks),
    )):
        brought[name] = pltpu.make_async_copy(src, dst, m_sem.at[n])
        brought[name].start()
    barrier = pltpu.get_barrier_semaphore()

    def greet(to):
        pl.semaphore_signal(barrier, inc=1, device_id=to, device_id_type=MESH)

    @pl.loop(1, NZ)
    def _(k):
        greet(((z + k) % NZ, j))

    def each_plane_peer(signal):
        for d in (1, 2, 3):
            signal(along(d))
            signal((z, device((x + d * c) % 4, (y + d * nc) % 4, nc)))

        @pl.loop(1, NEAR)
        def _(k):
            signal((z, to_user(k)[0]))

    each_plane_peer(greet)

    def vouch(to):
        pl.semaphore_signal(entered, inc=1, device_id=to, device_id_type=MESH)

    def own_start(n):
        own = pltpu.make_async_copy(zs.at[n, me], zr.at[n, me], z_recv.at[n])
        own.start()

    def to_users_start(n):
        own_start(n)

        @pl.loop(0, PEERS - 1)
        def _(k):
            z_to = plane(k // NEAR)
            j_to, slot = to_user(NEAR - 1 - k % NEAR)
            remote(
                zs.at[n, z_to * NEAR + slot], zr.at[n, me], z_send.at[n], z_recv.at[n], (z_to, j_to)
            )

    def to_holders_start(n):
        own_start(n)

        @pl.loop(0, PEERS - 1)
        def _(k):
            z_to = plane(k // NEAR)
            j_to, slot, there = to_holder(NEAR - 1 - k % NEAR)
            remote(
                zs.at[n, z_to * NEAR + slot], zr.at[n, z * NEAR + there],
                z_send.at[n], z_recv.at[n], (z_to, j_to),
            )

    def z_wait(n):
        await_bytes(zr.at[n], z_recv.at[n])

    def ag_start(n):
        for d in (2, 1, 3):
            remote(
                tables.at[n, pl.ds(0, 128)], tables.at[n, pl.ds((4 - d) * 128, 128)],
                ag_send.at[n], ag_recv.at[n], along(d),
            )

    def ag_wait(n):
        await_bytes(tables.at[n, pl.ds(128, 384)], ag_recv.at[n])

    def rs_start(n, zn):
        z_wait(zn)
        got = zr[zn].astype(F32)
        terms = jnp.concatenate(
            [got[:, :8].reshape(512, 128), got[:, 8:].reshape(512, 128)], axis=1
        ).astype(BF16)
        for d in (2, 1, 3, 0):
            part = jnp.dot(selt[pl.ds(d * 128, 128), :], terms, preferred_element_type=F32)
            if d:
                sb[n][d - 1] = part.astype(sb[n].dtype)
                remote(sb[n].at[d - 1], rb[n].at[d - 1], rs_send.at[n], rs_recv.at[n], along(d))
            else:
                pf[n % 2] = part

    def rs_end(n):
        await_bytes(rb[n], rs_recv.at[n])
        return pf[n % 2] + rb[n][0].astype(F32) + rb[n][1].astype(F32) + rb[n][2].astype(F32)

    def pack_terms(zn, terms):
        for f in range(8):
            relay[pl.ds(f, 128, stride=8), :] = terms[:, f * 128 : f * 128 + 128]
        zs[zn] = relay[...].reshape(PEERS, 16, 128).astype(BF16)

    def send_terms(zn, terms):
        pack_terms(zn, terms)
        to_holders_start(zn)

    def send_picks(zn, n):
        ag_wait(n)
        found = jnp.dot(sel[...], tables[n], preferred_element_type=F32)
        zs[zn] = jnp.concatenate(
            [found[:, :128].reshape(PEERS, 8, 128), found[:, 128:].reshape(PEERS, 8, 128)], axis=1
        ).astype(BF16)
        to_users_start(zn)

    def fetched(zn):
        z_wait(zn)
        relay[...] = zr[zn].astype(F32).reshape(1024, 128)
        return jnp.concatenate(
            [relay[pl.ds(f, 128, stride=8), :] for f in range(8)], axis=1
        ).astype(BF16)

    def to_users(rows):
        return lax.dot_general(rows, mat[...], NT, preferred_element_type=F32)

    def to_columns(rows):
        return jnp.dot(rows, mat[...], preferred_element_type=F32)

    def push_items(n, rows):
        tables[n, pl.ds(0, 128), :] = (scale_i[...] * rows).astype(BF16)
        ag_start(n)

    def build_picks(k):
        line = picks[pl.ds(k, 1), :]

        @pl.loop(0, 8)
        def _(r):
            at_row = pl.multiple_of(r * 128, 128)
            number = lax.broadcasted_iota(I32, (128, 1024), 0) + at_row
            oh[k, pl.ds(at_row, 128), :] = jnp.where(number == line, 1.0, 0.0).astype(BF16)

    for name in ("cols", "iemb", "ideg"):
        brought[name].wait()
    lane_row = lax.broadcasted_iota(I32, (1, 128), 1) & 7
    want = jnp.zeros((1, 128), I32)
    for f in range(8):
        want = jnp.where(lane_row == f, cols[:, f : f + 1], want)
    cs[...] = want
    cr[me] = want
    lane = lax.broadcasted_iota(I32, (16, 128), 1)
    row = lax.broadcasted_iota(I32, (16, 128), 0)
    some = lax.dot_general(
        jnp.where(lane == z * 16 + row, 1.0, 0.0).astype(BF16), iemb[...], NT,
        preferred_element_type=F32,
    )
    for blk in range(16):
        relay[pl.ds(blk * 16, 16), :] = some[:, blk * 128 : blk * 128 + 128]
    for q in range(NEAR):
        xs[q] = jnp.concatenate(
            [relay[pl.ds(q * 2 + e, 16, stride=16), :] for e in range(2)], axis=1
        ).astype(BF16)
    ds[...] = lax.rsqrt(ideg[...].astype(F32))

    for name in ("rows", "slots", "mask"):
        brought[name].wait()
    cell = slots[...] * 8 + rows[...]
    where = jnp.where(lax.broadcasted_iota(I32, (64, 32), 0) == cell, 1.0, 0.0).astype(BF16)
    lines = mask.reshape(32 * 128, 128)

    def add_blocks(first, last):
        @pl.loop(first, last)
        def _(group):
            for step in range(8):
                i = group * 8 + step
                line = lines[pl.ds(i, 32, stride=128), :].astype(F32).astype(BF16)
                sums = jnp.dot(where, line, preferred_element_type=F32)
                wide_mat[pl.ds(i, 64, stride=128), :] = sums

    add_blocks(0, 8)

    pl.semaphore_wait(barrier, NZ - 1 + NEAR - 1 + 6)

    own_x = pltpu.make_async_copy(xs.at[near], xr.at[near], x_sem.at[1])
    own_x.start()
    own_d = pltpu.make_async_copy(ds, dr.at[near], d_sem.at[1])
    own_d.start()

    @pl.loop(1, NEAR)
    def _(k):
        j_to, slot, there = to_holder(k)
        remote(xs.at[slot], xr.at[there], x_sem.at[0], x_sem.at[1], (z, j_to))
        remote(ds, dr.at[there], d_sem.at[0], d_sem.at[1], (z, j_to))

    each_plane_peer(vouch)
    add_blocks(8, 16)
    pl.semaphore_wait(entered, NEAR - 1 + 6)

    @pl.loop(0, PEERS - 1)
    def _(k):
        z_to = plane(k // NEAR)
        j_to, _, there = to_holder(NEAR - 1 - k % NEAR)
        remote(cs, cr.at[z * NEAR + there], c_sem.at[0], c_sem.at[1], (z_to, j_to))

    await_bytes(xr, x_sem.at[1])
    await_bytes(dr, d_sem.at[1])
    i0[...] = xr[...].astype(F32).reshape(128, 256)
    one_scale = dr[...].reshape(128, 128)
    scale_i[...] = jnp.concatenate([one_scale, one_scale], axis=1)
    push_items(0, i0[...])

    for f in range(8):
        mat[:, f * 128 : f * 128 + 128] = wide_mat[pl.ds(f * 1024, 1024), :].astype(BF16)
    eye = jnp.where(
        lax.broadcasted_iota(I32, (128, 128), 0) == lax.broadcasted_iota(I32, (128, 128), 1), 1.0, 0.0
    ).astype(BF16)
    brought["uemb"].wait()
    brought["udeg"].wait()
    user_rows = lax.dot_general(eye, uemb[...], NT, preferred_element_type=F32)
    u0[...] = user_rows
    scale_u[...] = lax.rsqrt(udeg[...].astype(F32))
    pack_terms(0, to_columns((scale_u[...] * user_rows).astype(BF16)))

    await_bytes(cr.at[pl.ds(0, PEERS - 1)], c_sem.at[1])
    col = cr[...]
    x_of = lax.shift_right_logical(col, jnp.full_like(col, 5)) & 3
    y_of = lax.shift_right_logical(col, jnp.full_like(col, 7))
    r_of, p_of = y_of * nc + x_of * c, x_of * nc + y_of * c
    place = (((r_of - r + 4) & 3) * 128 + p_of * 32 + (col & 31)).astype(F32)
    mine = (lax.broadcasted_iota(I32, (8, 128), 1) & 7) == lax.broadcasted_iota(I32, (8, 128), 0)
    spot = jnp.sum(
        jnp.where(mine[None], jnp.broadcast_to(place, (PEERS, 8, 128)), 0.0), axis=2, keepdims=True
    ) * (1.0 / 16.0)
    spot = jnp.broadcast_to(spot, (PEERS, 8, 128)).reshape(512, 128)
    for q in range(4):
        sel[:, q * 128 : q * 128 + 128] = jnp.where(
            spot == (lax.broadcasted_iota(I32, (512, 128), 1) + q * 128).astype(F32), 1.0, 0.0
        ).astype(BF16)
        turned = spot[q * 128 : q * 128 + 128].T
        for m in range(4):
            selt[m * 128 : m * 128 + 128, q * 128 : q * 128 + 128] = jnp.where(
                turned == (lax.broadcasted_iota(I32, (128, 128), 0) + m * 128).astype(F32), 1.0, 0.0
            ).astype(BF16)

    send_picks(1, 0)

    to_holders_start(0)
    brought["picks"].wait()
    build_picks(0)
    user_one = scale_u[...] * to_users(fetched(1))
    send_terms(2, to_columns((scale_u[...] * user_one).astype(BF16)))
    rs_start(0, 0)
    ufin[...] = u0[...] + user_one
    build_picks(1)
    item_one = scale_i[...] * rs_end(0)
    isum[...] = i0[...] + item_one
    push_items(1, item_one)

    rs_start(1, 2)
    send_picks(3, 1)
    item_final = (isum[...] + scale_i[...] * rs_end(1)) / 3.0
    tables[2, pl.ds(0, 128), :] = item_final.astype(BF16)
    ag_start(2)
    build_picks(2)
    send_picks(4, 2)
    build_picks(3)
    ufin[...] = (ufin[...] + scale_u[...] * to_users(fetched(3))) / 3.0

    final = fetched(4)
    exps = []
    for k in range(4):
        rows = jnp.dot(final, oh[k], preferred_element_type=F32)
        picked[k] = rows
        exps.append(jnp.exp(jnp.sum(ufin[...] * rows, axis=0, keepdims=True)))
    total = exps[0] + exps[1] + exps[2] + exps[3]
    slopes = [e / total - (1.0 if k == 0 else 0.0) for k, e in enumerate(exps)]
    spread = jnp.zeros((256, 1024), F32)
    for k in range(4):
        exact = slopes[k] * ufin[...]
        high = exact.astype(BF16)
        low = (exact - high.astype(F32)).astype(BF16)
        spread = spread + lax.dot_general(
            jnp.concatenate([high, low], axis=0), oh[k], NT, preferred_element_type=F32
        )
    send_terms(5, spread[:128] + spread[128:])
    grad = slopes[0] * picked[0]
    for k in range(1, 4):
        grad = grad + slopes[k] * picked[k]
    grad = grad / 3.0
    gu[...] = grad
    down_terms = to_columns((scale_u[...] * grad).astype(BF16))

    rs_start(2, 5)
    send_terms(6, down_terms)
    item_down = rs_end(2) / 3.0
    push_items(3, item_down)
    gi[...] = item_down
    send_picks(7, 3)
    rs_start(3, 6)
    first_item = scale_i[...] * rs_end(3)
    push_items(4, first_item)
    gi[...] = gi[...] + first_item
    first_user = scale_u[...] * to_users(fetched(7))
    send_terms(8, to_columns((scale_u[...] * first_user).astype(BF16)))
    gu[...] = gu[...] + first_user
    rs_start(4, 8)
    send_picks(9, 4)
    out_s[...] = (gi[...] + scale_i[...] * rs_end(4)).astype(BF16)
    own_o = pltpu.make_async_copy(
        out_s.at[pl.ds(pl.multiple_of(near * 16, 16), 16)], out_r.at[me], o_recv.at[2]
    )
    own_o.start()

    def out_step(z_to, k, arrival):
        j_to, slot = to_user(k)
        rows = pl.ds(pl.multiple_of(slot * 16, 16), 16)
        remote(out_s.at[rows], out_r.at[me], o_send.at[0], o_recv.at[arrival], (z_to, j_to))

    for d, arrival in ((2, 0), (6, 1), (1, 2), (7, 2)):

        @pl.loop(0, NEAR)
        def _(k):
            out_step((z + d) % NZ, k, arrival)

    @pl.loop(1, NEAR)
    def _(k):
        out_step(z, k, 2)

    def hand_on(d_from, first, count, d_to, sent, arrival):
        part = out_r.at[pl.ds((z + d_from) % NZ * NEAR + first, count)]
        remote(part, part, o_send.at[sent], o_recv.at[arrival], ((z + d_to) % NZ, j))

    await_bytes(out_r.at[pl.ds(0, 8)], o_recv.at[0])
    hand_on(6, 0, 8, 1, 1, 3)
    hand_on(6, 0, 4, 2, 2, 4)
    await_bytes(out_r.at[pl.ds(0, 8)], o_recv.at[1])
    hand_on(2, 0, 8, 7, 3, 5)
    hand_on(2, 4, 4, 6, 4, 6)
    gu_out[...] = gu[...] + scale_u[...] * to_users(fetched(9))
    await_bytes(out_r.at[pl.ds(0, 24)], o_recv.at[2])
    for arrival, count in ((3, 8), (5, 8), (4, 4), (6, 4)):
        await_bytes(out_r.at[pl.ds(0, count)], o_recv.at[arrival])

    @pl.loop(0, PEERS)
    def _(s):
        rows = out_r[s].astype(F32)
        for e in range(2):
            gi_out[pl.ds(s * 2 + e, 16, stride=128), :] = rows[:, e * 128 : e * 128 + 128]

    await_bytes(xs.at[pl.ds(0, NEAR - 1)], x_sem.at[0])
    await_bytes(dr.at[pl.ds(0, NEAR - 1)], d_sem.at[0])
    await_bytes(cr.at[pl.ds(0, PEERS - 1)], c_sem.at[0])
    await_bytes(out_r.at[pl.ds(0, 39)], o_send.at[0])
    for sent, count in ((1, 8), (2, 4), (3, 8), (4, 4)):
        await_bytes(out_r.at[pl.ds(0, count)], o_send.at[sent])
    for n in range(10):
        await_bytes(zs.at[n, pl.ds(0, PEERS - 1)], z_send.at[n])
    for n in range(5):
        await_bytes(tables.at[n, pl.ds(128, 384)], ag_send.at[n])
        await_bytes(rb[n], rs_send.at[n])


def on_device(
    user_emb, item_emb, user_deg, item_deg, blk_rows, blk_slot, fetch_cols, blk_mask, samples
):
    hbm = pl.BlockSpec(memory_space=pltpu.HBM)
    vmem = pl.BlockSpec(memory_space=pltpu.VMEM)
    dma = pltpu.SemaphoreType.DMA
    state = pltpu.VMEM((128, 256), F32)
    users = pltpu.VMEM((128, 1024), F32)
    gu_t, gi_t = pl.pallas_call(
        main_kernel,
        out_shape=(
            jax.ShapeDtypeStruct((128, 1024), F32),
            jax.ShapeDtypeStruct((2048, 128), F32),
        ),
        in_specs=[hbm] * 9,
        out_specs=(vmem, vmem),
        scratch_shapes=[
            users, pltpu.VMEM((1, 1024), F32), state, state, users, users, state, state,
            pltpu.VMEM((4, 1024, 1024), BF16), pltpu.VMEM((4, 128, 1024), F32),
            pltpu.VMEM((512, 512), BF16), pltpu.VMEM((512, 512), BF16),
            pltpu.VMEM((5, 512, 256), BF16),
            pltpu.VMEM((10, PEERS, 16, 128), BF16), pltpu.VMEM((10, PEERS, 16, 128), BF16),
            pltpu.VMEM((1, 128), I32), pltpu.VMEM((PEERS, 1, 128), I32),
            pltpu.VMEM((NEAR, 16, 256), BF16), pltpu.VMEM((NEAR, 16, 256), BF16),
            pltpu.VMEM((16, 128), F32), pltpu.VMEM((NEAR, 16, 128), F32),
            pltpu.VMEM((1024, 128), F32),
            pltpu.VMEM((8192, 128), F32), pltpu.VMEM((1024, 1024), BF16),
            pltpu.VMEM((1, 8), I32), pltpu.VMEM((1024, 128), BF16), pltpu.VMEM((2048, 128), BF16),
            pltpu.VMEM((1, 1024), I32), pltpu.VMEM((16, 128), I32), pltpu.VMEM((4, 1024), I32),
            pltpu.VMEM((1, 32), I32), pltpu.VMEM((1, 32), I32), pltpu.VMEM((32, 128, 128), I32),
            pltpu.VMEM((2, 128, 256), F32),
            *[pltpu.VMEM((3, 128, 256), t) for t in RS_TYPES],
            *[pltpu.VMEM((3, 128, 256), t) for t in RS_TYPES],
            pltpu.VMEM((128, 256), BF16), pltpu.VMEM((PEERS, 16, 256), BF16),
            dma((10,)), dma((10,)), dma((2,)), dma((2,)), dma((2,)),
            dma((5,)), dma((5,)), dma((5,)), dma((5,)), dma((5,)), dma((7,)), dma((9,)), pltpu.SemaphoreType.REGULAR,
        ],
        compiler_params=pltpu.CompilerParams(
            collective_id=0, has_side_effects=True, vmem_limit_bytes=56 * 2**20
        ),
        name="gcn",
    )(
        fetch_cols.reshape(1, -1), user_emb, item_emb, user_deg.reshape(1, -1), item_deg.reshape(16, 128),
        samples.T, blk_rows.reshape(1, -1), blk_slot.reshape(1, -1), blk_mask,
    )
    return pl.pallas_call(
        finish_kernel,
        grid=(4,),
        out_shape=(
            jax.ShapeDtypeStruct((1024, 128), F32),
            jax.ShapeDtypeStruct((2048, 128), F32),
        ),
        in_specs=[
            pl.BlockSpec((128, 256), lambda i: (0, i)),
            pl.BlockSpec((512, 128), lambda i: (i, 0)),
        ],
        out_specs=(
            pl.BlockSpec((256, 128), lambda i: (i, 0)),
            pl.BlockSpec((512, 128), lambda i: (i, 0)),
        ),
        compiler_params=pltpu.CompilerParams(vmem_limit_bytes=56 * 2**20),
        name="finish",
    )(gu_t, gi_t)


def solution(mesh):
    both = ("ugrp", "item")
    return jax.shard_map(
        on_device,
        mesh=mesh,
        in_specs=(
            P(both, None), P("item", None), P(both), P("item"), P(both), P(both), P(both),
            P(both, None, None), P(both, None),
        ),
        out_specs=(P(both, None), P("item", None)),
        check_vma=False,
    )
```

```python
import jax
import jax.numpy as jnp
from jax import lax
from jax.experimental import pallas as pl
from jax.experimental.pallas import tpu as pltpu
from jax.sharding import PartitionSpec as P

F32, BF16, I32 = jnp.float32, jnp.bfloat16, jnp.int32
MESH = pl.DeviceIdType.MESH
NT = (((1,), (1,)), ((), ()))
NZ, PEERS, NEAR = 8, 64, 8
RS_TYPES = (BF16, BF16, F32, BF16, BF16)


def finish_kernel(gu_in, gi_in, gu_out, gi_out, gu_t, gi_t, gu, gi, came, left):
    parts = [pl.ds(i * 512, 512) for i in range(4)]
    loads = [pltpu.make_async_copy(gi_in.at[p], gi_t.at[p], came.at[i]) for i, p in enumerate(parts)]
    loads.append(pltpu.make_async_copy(gu_in, gu_t, came.at[4]))
    stores = [pltpu.make_async_copy(gi.at[p], gi_out.at[p], left.at[i]) for i, p in enumerate(parts)]
    stores.append(pltpu.make_async_copy(gu, gu_out, left.at[4]))
    for load in loads:
        load.start()
    for i in range(4):
        loads[i].wait()
        for blk in range(4):
            rows = pl.ds(i * 512 + blk * 128, 128)
            gi[rows, :] = gi_t[rows, :].T
        stores[i].start()
    loads[4].wait()
    gu[...] = gu_t[...].T
    stores[4].start()
    for store in stores:
        store.wait()


def main_kernel(
    cols_in, uemb_in, iemb_in, udeg_in, ideg_in, picks_in, rows_in, slots_in, mask_in,
    gu_out, gi_out,
    u0, scale_u, i0, scale_i, ufin, gu, gi, isum,
    oh, picked, sel, selt, tables, zs, zr, cs, cz, cr, xs, xr, ds, dr, relay, wide_mat, mat,
    cols, uemb, iemb, udeg, ideg, picks, rows, slots, mask,
    pf, sb0, sb1, sb2, sb3, sb4, rb0, rb1, rb2, rb3, rb4, out_s, out_r,
    z_send, z_recv, c_sem, e_sem, x_sem, d_sem, ag_send, ag_recv, rs_send, rs_recv, o_send, o_recv, m_sem, entered,
):
    sb, rb = (sb0, sb1, sb2, sb3, sb4), (rb0, rb1, rb2, rb3, rb4)
    z, j = lax.axis_index("ugrp"), lax.axis_index("item")
    c = j % 2
    x, y = (j // 2) % 4, j // 8
    nc = 1 - c
    p, r = x * nc + y * c, y * nc + x * c
    near = p * 2 + c
    me = z * NEAR + near

    def device(x_to, y_to, c_to):
        return (y_to * 4 + x_to) * 2 + c_to

    def along(d):
        r_to = (r + d) % 4
        return (z, device(p * nc + r_to * c, r_to * nc + p * c, c))

    def offset(k):
        return (p + k // 2) % 4, (c + k % 2) % 2

    def plane(i):
        return (z + 4 + ((i + 1) // 2) * (1 - 2 * (i % 2))) % NZ

    def to_user(k):
        p_to, c_to = offset(k)
        return device(p_to * nc + x * c, y * nc + p_to * c, c_to), p_to * 2 + c_to

    def to_holder(k):
        p_to, c_to = offset(k)
        j_to = device(p_to * (1 - c_to) + x * c_to, y * (1 - c_to) + p_to * c_to, c_to)
        return j_to, p_to * 2 + c_to, (x * (1 - c_to) + y * c_to) * 2 + c

    def remote(src, dst, send, recv, to):
        pltpu.make_async_remote_copy(
            src_ref=src, dst_ref=dst, send_sem=send, recv_sem=recv, device_id=to, device_id_type=MESH
        ).start()

    def await_bytes(ref, sem):
        pltpu.make_async_copy(ref, ref, sem).wait()

    brought = {}
    for n, (name, src, dst) in enumerate((
        ("iemb", iemb_in, iemb), ("ideg", ideg_in, ideg), ("cols", cols_in, cols),
        ("uemb", uemb_in, uemb), ("udeg", udeg_in, udeg), ("rows", rows_in, rows),
        ("slots", slots_in, slots), ("mask", mask_in, mask), ("picks", picks_in, picks),
    )):
        brought[name] = pltpu.make_async_copy(src, dst, m_sem.at[n])
        brought[name].start()
    barrier = pltpu.get_barrier_semaphore()

    def greet(to):
        pl.semaphore_signal(barrier, inc=1, device_id=to, device_id_type=MESH)

    @pl.loop(1, NZ)
    def _(k):
        greet(((z + k) % NZ, j))

    def each_plane_peer(signal):
        for d in (1, 2, 3):
            signal(along(d))
            signal((z, device((x + d * c) % 4, (y + d * nc) % 4, nc)))

        @pl.loop(1, NEAR)
        def _(k):
            signal((z, to_user(k)[0]))

    each_plane_peer(greet)

    def vouch(to):
        pl.semaphore_signal(entered, inc=1, device_id=to, device_id_type=MESH)

    def own_start(n):
        own = pltpu.make_async_copy(zs.at[n, me], zr.at[n, me], z_recv.at[n])
        own.start()

    def to_users_start(n):
        own_start(n)

        @pl.loop(0, PEERS - 1)
        def _(k):
            z_to = plane(k // NEAR)
            j_to, slot = to_user(NEAR - 1 - k % NEAR)
            remote(
                zs.at[n, z_to * NEAR + slot], zr.at[n, me], z_send.at[n], z_recv.at[n], (z_to, j_to)
            )

    def to_holders_start(n):
        own_start(n)

        @pl.loop(0, PEERS - 1)
        def _(k):
            z_to = plane(k // NEAR)
            j_to, slot, there = to_holder(NEAR - 1 - k % NEAR)
            remote(
                zs.at[n, z_to * NEAR + slot], zr.at[n, z * NEAR + there],
                z_send.at[n], z_recv.at[n], (z_to, j_to),
            )

    def z_wait(n):
        await_bytes(zr.at[n], z_recv.at[n])

    def ag_start(n):
        for d in (2, 1, 3):
            remote(
                tables.at[n, pl.ds(0, 128)], tables.at[n, pl.ds((4 - d) * 128, 128)],
                ag_send.at[n], ag_recv.at[n], along(d),
            )

    def ag_wait(n):
        await_bytes(tables.at[n, pl.ds(128, 384)], ag_recv.at[n])

    def rs_start(n, zn):
        z_wait(zn)
        got = zr[zn].astype(F32)
        terms = jnp.concatenate(
            [got[:, :8].reshape(512, 128), got[:, 8:].reshape(512, 128)], axis=1
        ).astype(BF16)
        for d in (2, 1, 3, 0):
            part = jnp.dot(selt[pl.ds(d * 128, 128), :], terms, preferred_element_type=F32)
            if d:
                sb[n][d - 1] = part.astype(sb[n].dtype)
                remote(sb[n].at[d - 1], rb[n].at[d - 1], rs_send.at[n], rs_recv.at[n], along(d))
            else:
                pf[n % 2] = part

    def rs_end(n):
        await_bytes(rb[n], rs_recv.at[n])
        return pf[n % 2] + rb[n][0].astype(F32) + rb[n][1].astype(F32) + rb[n][2].astype(F32)

    def pack_terms(zn, terms):
        for f in range(8):
            relay[pl.ds(f, 128, stride=8), :] = terms[:, f * 128 : f * 128 + 128]
        zs[zn] = relay[...].reshape(PEERS, 16, 128).astype(BF16)

    def send_terms(zn, terms):
        pack_terms(zn, terms)
        to_holders_start(zn)

    def send_picks(zn, n):
        ag_wait(n)
        found = jnp.dot(sel[...], tables[n], preferred_element_type=F32)
        zs[zn] = jnp.concatenate(
            [found[:, :128].reshape(PEERS, 8, 128), found[:, 128:].reshape(PEERS, 8, 128)], axis=1
        ).astype(BF16)
        to_users_start(zn)

    def fetched(zn):
        z_wait(zn)
        relay[...] = zr[zn].astype(F32).reshape(1024, 128)
        return jnp.concatenate(
            [relay[pl.ds(f, 128, stride=8), :] for f in range(8)], axis=1
        ).astype(BF16)

    def to_users(rows):
        return lax.dot_general(rows, mat[...], NT, preferred_element_type=F32)

    def to_columns(rows):
        return jnp.dot(rows, mat[...], preferred_element_type=F32)

    def push_items(n, rows):
        tables[n, pl.ds(0, 128), :] = (scale_i[...] * rows).astype(BF16)
        ag_start(n)

    def build_picks(k):
        line = picks[pl.ds(k, 1), :]

        @pl.loop(0, 8)
        def _(r):
            at_row = pl.multiple_of(r * 128, 128)
            number = lax.broadcasted_iota(I32, (128, 1024), 0) + at_row
            oh[k, pl.ds(at_row, 128), :] = jnp.where(number == line, 1.0, 0.0).astype(BF16)

    for name in ("cols", "iemb", "ideg"):
        brought[name].wait()
    lane_row = lax.broadcasted_iota(I32, (1, 128), 1) & 7
    want = jnp.zeros((1, 128), I32)
    for f in range(8):
        want = jnp.where(lane_row == f, cols[:, f : f + 1], want)
    cs[...] = want
    cz[z] = want
    lane = lax.broadcasted_iota(I32, (16, 128), 1)
    row = lax.broadcasted_iota(I32, (16, 128), 0)
    some = lax.dot_general(
        jnp.where(lane == z * 16 + row, 1.0, 0.0).astype(BF16), iemb[...], NT,
        preferred_element_type=F32,
    )
    for blk in range(16):
        relay[pl.ds(blk * 16, 16), :] = some[:, blk * 128 : blk * 128 + 128]
    for q in range(NEAR):
        xs[q] = jnp.concatenate(
            [relay[pl.ds(q * 2 + e, 16, stride=16), :] for e in range(2)], axis=1
        ).astype(BF16)
    ds[...] = lax.rsqrt(ideg[...].astype(F32))

    for name in ("rows", "slots", "mask"):
        brought[name].wait()
    cell = slots[...] * 8 + rows[...]
    where = jnp.where(lax.broadcasted_iota(I32, (64, 32), 0) == cell, 1.0, 0.0).astype(BF16)
    lines = mask.reshape(32 * 128, 128)

    def add_blocks(first, last):
        @pl.loop(first, last)
        def _(group):
            for step in range(8):
                i = group * 8 + step
                line = lines[pl.ds(i, 32, stride=128), :].astype(F32).astype(BF16)
                sums = jnp.dot(where, line, preferred_element_type=F32)
                wide_mat[pl.ds(i, 64, stride=128), :] = sums

    add_blocks(0, 8)

    pl.semaphore_wait(barrier, NZ - 1 + NEAR - 1 + 6)

    own_x = pltpu.make_async_copy(xs.at[near], xr.at[near], x_sem.at[1])
    own_x.start()
    own_d = pltpu.make_async_copy(ds, dr.at[near], d_sem.at[1])
    own_d.start()

    @pl.loop(1, NEAR)
    def _(k):
        j_to, slot, there = to_holder(k)
        remote(xs.at[slot], xr.at[there], x_sem.at[0], x_sem.at[1], (z, j_to))
        remote(ds, dr.at[there], d_sem.at[0], d_sem.at[1], (z, j_to))

    @pl.loop(1, NZ)
    def _(k):
        remote(cs, cz.at[z], c_sem.at[0], c_sem.at[1], ((z + k) % NZ, j))

    each_plane_peer(vouch)
    add_blocks(8, 16)
    await_bytes(xr, x_sem.at[1])
    await_bytes(dr, d_sem.at[1])
    i0[...] = xr[...].astype(F32).reshape(128, 256)
    one_scale = dr[...].reshape(128, 128)
    scale_i[...] = jnp.concatenate([one_scale, one_scale], axis=1)
    push_items(0, i0[...])

    await_bytes(cz.at[pl.ds(0, NZ - 1)], c_sem.at[1])
    own_c = pltpu.make_async_copy(cz, cr.at[near], e_sem.at[1])
    own_c.start()

    @pl.loop(1, NEAR)
    def _(k):
        j_to, _, there = to_holder(k)
        remote(cz, cr.at[there], e_sem.at[0], e_sem.at[1], (z, j_to))

    for f in range(8):
        mat[:, f * 128 : f * 128 + 128] = wide_mat[pl.ds(f * 1024, 1024), :].astype(BF16)
    eye = jnp.where(
        lax.broadcasted_iota(I32, (128, 128), 0) == lax.broadcasted_iota(I32, (128, 128), 1), 1.0, 0.0
    ).astype(BF16)
    brought["uemb"].wait()
    brought["udeg"].wait()
    user_rows = lax.dot_general(eye, uemb[...], NT, preferred_element_type=F32)
    u0[...] = user_rows
    scale_u[...] = lax.rsqrt(udeg[...].astype(F32))
    pack_terms(0, to_columns((scale_u[...] * user_rows).astype(BF16)))
    pl.semaphore_wait(entered, NEAR - 1 + 6)
    to_holders_start(0)

    await_bytes(cr, e_sem.at[1])
    col = jnp.stack([cr[:, k] for k in range(NZ)], axis=0).reshape(PEERS, 1, 128)
    x_of = lax.shift_right_logical(col, jnp.full_like(col, 5)) & 3
    y_of = lax.shift_right_logical(col, jnp.full_like(col, 7))
    r_of, p_of = y_of * nc + x_of * c, x_of * nc + y_of * c
    place = (((r_of - r + 4) & 3) * 128 + p_of * 32 + (col & 31)).astype(F32)
    mine = (lax.broadcasted_iota(I32, (8, 128), 1) & 7) == lax.broadcasted_iota(I32, (8, 128), 0)
    spot = jnp.sum(
        jnp.where(mine[None], jnp.broadcast_to(place, (PEERS, 8, 128)), 0.0), axis=2, keepdims=True
    ) * (1.0 / 16.0)
    spot = jnp.broadcast_to(spot, (PEERS, 8, 128)).reshape(512, 128)
    for q in range(4):
        sel[:, q * 128 : q * 128 + 128] = jnp.where(
            spot == (lax.broadcasted_iota(I32, (512, 128), 1) + q * 128).astype(F32), 1.0, 0.0
        ).astype(BF16)
        turned = spot[q * 128 : q * 128 + 128].T
        for m in range(4):
            selt[m * 128 : m * 128 + 128, q * 128 : q * 128 + 128] = jnp.where(
                turned == (lax.broadcasted_iota(I32, (128, 128), 0) + m * 128).astype(F32), 1.0, 0.0
            ).astype(BF16)

    send_picks(1, 0)
    brought["picks"].wait()
    build_picks(0)
    user_one = scale_u[...] * to_users(fetched(1))
    send_terms(2, to_columns((scale_u[...] * user_one).astype(BF16)))
    rs_start(0, 0)
    ufin[...] = u0[...] + user_one
    build_picks(1)
    item_one = scale_i[...] * rs_end(0)
    isum[...] = i0[...] + item_one
    push_items(1, item_one)

    rs_start(1, 2)
    send_picks(3, 1)
    item_final = (isum[...] + scale_i[...] * rs_end(1)) / 3.0
    tables[2, pl.ds(0, 128), :] = item_final.astype(BF16)
    ag_start(2)
    build_picks(2)
    send_picks(4, 2)
    build_picks(3)
    ufin[...] = (ufin[...] + scale_u[...] * to_users(fetched(3))) / 3.0

    final = fetched(4)
    exps = []
    for k in range(4):
        rows = jnp.dot(final, oh[k], preferred_element_type=F32)
        picked[k] = rows
        exps.append(jnp.exp(jnp.sum(ufin[...] * rows, axis=0, keepdims=True)))
    total = exps[0] + exps[1] + exps[2] + exps[3]
    slopes = [e / total - (1.0 if k == 0 else 0.0) for k, e in enumerate(exps)]
    spread = jnp.zeros((256, 1024), F32)
    for k in range(4):
        exact = slopes[k] * ufin[...]
        high = exact.astype(BF16)
        low = (exact - high.astype(F32)).astype(BF16)
        spread = spread + lax.dot_general(
            jnp.concatenate([high, low], axis=0), oh[k], NT, preferred_element_type=F32
        )
    send_terms(5, spread[:128] + spread[128:])
    grad = slopes[0] * picked[0]
    for k in range(1, 4):
        grad = grad + slopes[k] * picked[k]
    grad = grad / 3.0
    gu[...] = grad
    down_terms = to_columns((scale_u[...] * grad).astype(BF16))

    rs_start(2, 5)
    send_terms(6, down_terms)
    item_down = rs_end(2) / 3.0
    push_items(3, item_down)
    gi[...] = item_down
    send_picks(7, 3)
    rs_start(3, 6)
    first_item = scale_i[...] * rs_end(3)
    push_items(4, first_item)
    gi[...] = gi[...] + first_item
    first_user = scale_u[...] * to_users(fetched(7))
    send_terms(8, to_columns((scale_u[...] * first_user).astype(BF16)))
    gu[...] = gu[...] + first_user
    send_picks(9, 4)
    rs_start(4, 8)
    out_s[...] = (gi[...] + scale_i[...] * rs_end(4)).astype(BF16)
    own_o = pltpu.make_async_copy(
        out_s.at[pl.ds(pl.multiple_of(near * 16, 16), 16)], out_r.at[me], o_recv.at[2]
    )
    own_o.start()

    def out_step(z_to, k, arrival):
        j_to, slot = to_user(k)
        rows = pl.ds(pl.multiple_of(slot * 16, 16), 16)
        remote(out_s.at[rows], out_r.at[me], o_send.at[0], o_recv.at[arrival], (z_to, j_to))

    for d, arrival in ((2, 0), (6, 1), (1, 2), (7, 2)):

        @pl.loop(0, NEAR)
        def _(k):
            out_step((z + d) % NZ, k, arrival)

    @pl.loop(1, NEAR)
    def _(k):
        out_step(z, k, 2)

    def hand_on(d_from, first, count, d_to, sent, arrival):
        part = out_r.at[pl.ds((z + d_from) % NZ * NEAR + first, count)]
        remote(part, part, o_send.at[sent], o_recv.at[arrival], ((z + d_to) % NZ, j))

    await_bytes(out_r.at[pl.ds(0, 8)], o_recv.at[0])
    hand_on(6, 0, 8, 1, 1, 3)
    hand_on(6, 0, 4, 2, 2, 4)
    await_bytes(out_r.at[pl.ds(0, 8)], o_recv.at[1])
    hand_on(2, 0, 8, 7, 3, 5)
    hand_on(2, 4, 4, 6, 4, 6)
    gu_out[...] = gu[...] + scale_u[...] * to_users(fetched(9))
    await_bytes(out_r.at[pl.ds(0, 24)], o_recv.at[2])
    for arrival, count in ((3, 8), (5, 8), (4, 4), (6, 4)):
        await_bytes(out_r.at[pl.ds(0, count)], o_recv.at[arrival])

    @pl.loop(0, PEERS)
    def _(s):
        rows = out_r[s].astype(F32)
        for e in range(2):
            gi_out[pl.ds(s * 2 + e, 16, stride=128), :] = rows[:, e * 128 : e * 128 + 128]

    await_bytes(xs.at[pl.ds(0, NEAR - 1)], x_sem.at[0])
    await_bytes(dr.at[pl.ds(0, NEAR - 1)], d_sem.at[0])
    await_bytes(cz.at[pl.ds(0, NZ - 1)], c_sem.at[0])
    await_bytes(cr.at[pl.ds(0, NEAR - 1)], e_sem.at[0])
    await_bytes(out_r.at[pl.ds(0, 39)], o_send.at[0])
    for sent, count in ((1, 8), (2, 4), (3, 8), (4, 4)):
        await_bytes(out_r.at[pl.ds(0, count)], o_send.at[sent])
    for n in range(10):
        await_bytes(zs.at[n, pl.ds(0, PEERS - 1)], z_send.at[n])
    for n in range(5):
        await_bytes(tables.at[n, pl.ds(128, 384)], ag_send.at[n])
        await_bytes(rb[n], rs_send.at[n])


def on_device(
    user_emb, item_emb, user_deg, item_deg, blk_rows, blk_slot, fetch_cols, blk_mask, samples
):
    hbm = pl.BlockSpec(memory_space=pltpu.HBM)
    vmem = pl.BlockSpec(memory_space=pltpu.VMEM)
    dma = pltpu.SemaphoreType.DMA
    state = pltpu.VMEM((128, 256), F32)
    users = pltpu.VMEM((128, 1024), F32)
    gu_t, gi_t = pl.pallas_call(
        main_kernel,
        out_shape=(
            jax.ShapeDtypeStruct((128, 1024), F32),
            jax.ShapeDtypeStruct((2048, 128), F32),
        ),
        in_specs=[hbm] * 9,
        out_specs=(vmem, vmem),
        scratch_shapes=[
            users, pltpu.VMEM((1, 1024), F32), state, state, users, users, state, state,
            pltpu.VMEM((4, 1024, 1024), BF16), pltpu.VMEM((4, 128, 1024), F32),
            pltpu.VMEM((512, 512), BF16), pltpu.VMEM((512, 512), BF16),
            pltpu.VMEM((5, 512, 256), BF16),
            pltpu.VMEM((10, PEERS, 16, 128), BF16), pltpu.VMEM((10, PEERS, 16, 128), BF16),
            pltpu.VMEM((1, 128), I32), pltpu.VMEM((NZ, 1, 128), I32), pltpu.VMEM((NEAR, NZ, 1, 128), I32),
            pltpu.VMEM((NEAR, 16, 256), BF16), pltpu.VMEM((NEAR, 16, 256), BF16),
            pltpu.VMEM((16, 128), F32), pltpu.VMEM((NEAR, 16, 128), F32),
            pltpu.VMEM((1024, 128), F32),
            pltpu.VMEM((8192, 128), F32), pltpu.VMEM((1024, 1024), BF16),
            pltpu.VMEM((1, 8), I32), pltpu.VMEM((1024, 128), BF16), pltpu.VMEM((2048, 128), BF16),
            pltpu.VMEM((1, 1024), I32), pltpu.VMEM((16, 128), I32), pltpu.VMEM((4, 1024), I32),
            pltpu.VMEM((1, 32), I32), pltpu.VMEM((1, 32), I32), pltpu.VMEM((32, 128, 128), I32),
            pltpu.VMEM((2, 128, 256), F32),
            *[pltpu.VMEM((3, 128, 256), t) for t in RS_TYPES],
            *[pltpu.VMEM((3, 128, 256), t) for t in RS_TYPES],
            pltpu.VMEM((128, 256), BF16), pltpu.VMEM((PEERS, 16, 256), BF16),
            dma((10,)), dma((10,)), dma((2,)), dma((2,)), dma((2,)), dma((2,)),
            dma((5,)), dma((5,)), dma((5,)), dma((5,)), dma((5,)), dma((7,)), dma((9,)), pltpu.SemaphoreType.REGULAR,
        ],
        compiler_params=pltpu.CompilerParams(
            collective_id=0, has_side_effects=True, vmem_limit_bytes=56 * 2**20
        ),
        name="gcn",
    )(
        fetch_cols.reshape(1, -1), user_emb, item_emb, user_deg.reshape(1, -1), item_deg.reshape(16, 128),
        samples.T, blk_rows.reshape(1, -1), blk_slot.reshape(1, -1), blk_mask,
    )
    return pl.pallas_call(
        finish_kernel,
        out_shape=(
            jax.ShapeDtypeStruct((1024, 128), F32),
            jax.ShapeDtypeStruct((2048, 128), F32),
        ),
        in_specs=[pl.BlockSpec(memory_space=pl.ANY)] * 2,
        out_specs=(pl.BlockSpec(memory_space=pl.ANY), pl.BlockSpec(memory_space=pl.ANY)),
        scratch_shapes=[
            users, pltpu.VMEM((2048, 128), F32), pltpu.VMEM((1024, 128), F32),
            pltpu.VMEM((2048, 128), F32), dma((5,)), dma((5,)),
        ],
        compiler_params=pltpu.CompilerParams(vmem_limit_bytes=56 * 2**20),
        name="finish",
    )(gu_t, gi_t)


def solution(mesh):
    both = ("ugrp", "item")
    return jax.shard_map(
        on_device,
        mesh=mesh,
        in_specs=(
            P(both, None), P("item", None), P(both), P("item"), P(both), P(both), P(both),
            P(both, None, None), P(both, None),
        ),
        out_specs=(P(both, None), P("item", None)),
        check_vma=False,
    )
```

```python
import jax
import jax.numpy as jnp
from jax import lax
from jax.experimental import pallas as pl
from jax.experimental.pallas import tpu as pltpu
from jax.sharding import PartitionSpec as P

F32, BF16, I32 = jnp.float32, jnp.bfloat16, jnp.int32
MESH = pl.DeviceIdType.MESH
NT = (((1,), (1,)), ((), ()))
NZ, PEERS, NEAR = 8, 64, 8
RS_TYPES = (BF16, BF16, F32, BF16, BF16)


def finish_kernel(gu_in, gi_in, gu_out, gi_out, gu_t, gi_t, gu, gi, came, left):
    parts = [pl.ds(i * 512, 512) for i in range(4)]
    loads = [pltpu.make_async_copy(gi_in.at[p], gi_t.at[p], came.at[i]) for i, p in enumerate(parts)]
    loads.append(pltpu.make_async_copy(gu_in, gu_t, came.at[4]))
    stores = [pltpu.make_async_copy(gi.at[p], gi_out.at[p], left.at[i]) for i, p in enumerate(parts)]
    stores.append(pltpu.make_async_copy(gu, gu_out, left.at[4]))
    for load in loads:
        load.start()
    for i in range(4):
        loads[i].wait()
        for blk in range(4):
            rows = pl.ds(i * 512 + blk * 128, 128)
            gi[rows, :] = gi_t[rows, :].T
        stores[i].start()
    loads[4].wait()
    gu[...] = gu_t[...].T
    stores[4].start()
    for store in stores:
        store.wait()


def main_kernel(
    cols_in, uemb_in, iemb_in, udeg_in, ideg_in, picks_in, rows_in, slots_in, mask_in,
    gu_out, gi_out,
    u0, scale_u, i0, scale_i, ufin, gu, gi, isum,
    oh, picked, sel, selt, tables, zs, zr, cs, cz, cr, xs, xr, ds, dr, relay, wide_mat, mat,
    cols, uemb, iemb, udeg, ideg, picks, rows, slots, mask,
    pf, sb0, sb1, sb2, sb3, sb4, rb0, rb1, rb2, rb3, rb4, out_s, out_r,
    z_send, z_recv, c_sem, e_sem, x_sem, d_sem, ag_send, ag_recv, rs_send, rs_recv, o_send, o_recv, m_sem, entered,
):
    sb, rb = (sb0, sb1, sb2, sb3, sb4), (rb0, rb1, rb2, rb3, rb4)
    z, j = lax.axis_index("ugrp"), lax.axis_index("item")
    c = j % 2
    x, y = (j // 2) % 4, j // 8
    nc = 1 - c
    p, r = x * nc + y * c, y * nc + x * c
    near = p * 2 + c
    me = z * NEAR + near

    def device(x_to, y_to, c_to):
        return (y_to * 4 + x_to) * 2 + c_to

    def along(d):
        r_to = (r + d) % 4
        return (z, device(p * nc + r_to * c, r_to * nc + p * c, c))

    def offset(k):
        return (p + k // 2) % 4, (c + k % 2) % 2

    def plane(i):
        return (z + 4 + ((i + 1) // 2) * (1 - 2 * (i % 2))) % NZ

    def to_user(k):
        p_to, c_to = offset(k)
        return device(p_to * nc + x * c, y * nc + p_to * c, c_to), p_to * 2 + c_to

    def to_holder(k):
        p_to, c_to = offset(k)
        j_to = device(p_to * (1 - c_to) + x * c_to, y * (1 - c_to) + p_to * c_to, c_to)
        return j_to, p_to * 2 + c_to, (x * (1 - c_to) + y * c_to) * 2 + c

    def remote(src, dst, send, recv, to):
        pltpu.make_async_remote_copy(
            src_ref=src, dst_ref=dst, send_sem=send, recv_sem=recv, device_id=to, device_id_type=MESH
        ).start()

    def await_bytes(ref, sem):
        pltpu.make_async_copy(ref, ref, sem).wait()

    brought = {}
    for n, (name, src, dst) in enumerate((
        ("iemb", iemb_in, iemb), ("ideg", ideg_in, ideg), ("cols", cols_in, cols),
        ("uemb", uemb_in, uemb), ("udeg", udeg_in, udeg), ("rows", rows_in, rows),
        ("slots", slots_in, slots), ("mask", mask_in, mask), ("picks", picks_in, picks),
    )):
        brought[name] = pltpu.make_async_copy(src, dst, m_sem.at[n])
        brought[name].start()
    barrier = pltpu.get_barrier_semaphore()

    def greet(to):
        pl.semaphore_signal(barrier, inc=1, device_id=to, device_id_type=MESH)

    @pl.loop(1, NZ)
    def _(k):
        greet(((z + k) % NZ, j))

    def each_plane_peer(signal):
        for d in (1, 2, 3):
            signal(along(d))
            signal((z, device((x + d * c) % 4, (y + d * nc) % 4, nc)))

        @pl.loop(1, NEAR)
        def _(k):
            signal((z, to_user(k)[0]))

    each_plane_peer(greet)

    def vouch(to):
        pl.semaphore_signal(entered, inc=1, device_id=to, device_id_type=MESH)

    def own_start(n):
        own = pltpu.make_async_copy(zs.at[n, me], zr.at[n, me], z_recv.at[n])
        own.start()

    def to_users_start(n):
        own_start(n)

        @pl.loop(0, PEERS - 1)
        def _(k):
            z_to = plane(k // NEAR)
            j_to, slot = to_user(NEAR - 1 - k % NEAR)
            remote(
                zs.at[n, z_to * NEAR + slot], zr.at[n, me], z_send.at[n], z_recv.at[n], (z_to, j_to)
            )

    def to_holders_start(n):
        own_start(n)

        @pl.loop(0, PEERS - 1)
        def _(k):
            z_to = plane(k // NEAR)
            j_to, slot, there = to_holder(NEAR - 1 - k % NEAR)
            remote(
                zs.at[n, z_to * NEAR + slot], zr.at[n, z * NEAR + there],
                z_send.at[n], z_recv.at[n], (z_to, j_to),
            )

    def z_wait(n):
        await_bytes(zr.at[n], z_recv.at[n])

    def ag_start(n):
        for d in (2, 1, 3):
            remote(
                tables.at[n, pl.ds(0, 128)], tables.at[n, pl.ds((4 - d) * 128, 128)],
                ag_send.at[n], ag_recv.at[n], along(d),
            )

    def ag_wait(n):
        await_bytes(tables.at[n, pl.ds(128, 384)], ag_recv.at[n])

    def rs_start(n, zn):
        z_wait(zn)
        got = zr[zn].astype(F32)
        terms = jnp.concatenate(
            [got[:, :8].reshape(512, 128), got[:, 8:].reshape(512, 128)], axis=1
        ).astype(BF16)
        for d in (2, 1, 3, 0):
            part = jnp.dot(selt[pl.ds(d * 128, 128), :], terms, preferred_element_type=F32)
            if d:
                sb[n][d - 1] = part.astype(sb[n].dtype)
                remote(sb[n].at[d - 1], rb[n].at[d - 1], rs_send.at[n], rs_recv.at[n], along(d))
            else:
                pf[n % 2] = part

    def rs_end(n):
        await_bytes(rb[n], rs_recv.at[n])
        return pf[n % 2] + rb[n][0].astype(F32) + rb[n][1].astype(F32) + rb[n][2].astype(F32)

    def pack_terms(zn, terms):
        for f in range(8):
            relay[pl.ds(f, 128, stride=8), :] = terms[:, f * 128 : f * 128 + 128]
        zs[zn] = relay[...].reshape(PEERS, 16, 128).astype(BF16)

    def send_terms(zn, terms):
        pack_terms(zn, terms)
        to_holders_start(zn)

    def send_picks(zn, n):
        ag_wait(n)
        found = jnp.dot(sel[...], tables[n], preferred_element_type=F32)
        zs[zn] = jnp.concatenate(
            [found[:, :128].reshape(PEERS, 8, 128), found[:, 128:].reshape(PEERS, 8, 128)], axis=1
        ).astype(BF16)
        to_users_start(zn)

    def fetched(zn):
        z_wait(zn)
        relay[...] = zr[zn].astype(F32).reshape(1024, 128)
        return jnp.concatenate(
            [relay[pl.ds(f, 128, stride=8), :] for f in range(8)], axis=1
        ).astype(BF16)

    def to_users(rows):
        return lax.dot_general(rows, mat[...], NT, preferred_element_type=F32)

    def to_columns(rows):
        return jnp.dot(rows, mat[...], preferred_element_type=F32)

    def push_items(n, rows):
        tables[n, pl.ds(0, 128), :] = (scale_i[...] * rows).astype(BF16)
        ag_start(n)

    def build_picks(k):
        line = picks[pl.ds(k, 1), :]

        @pl.loop(0, 8)
        def _(r):
            at_row = pl.multiple_of(r * 128, 128)
            number = lax.broadcasted_iota(I32, (128, 1024), 0) + at_row
            oh[pl.ds(at_row, 128), k * 1024 : k * 1024 + 1024] = jnp.where(number == line, 1.0, 0.0).astype(BF16)

    for name in ("cols", "iemb", "ideg"):
        brought[name].wait()
    lane_row = lax.broadcasted_iota(I32, (1, 128), 1) & 7
    want = jnp.zeros((1, 128), I32)
    for f in range(8):
        want = jnp.where(lane_row == f, cols[:, f : f + 1], want)
    cs[...] = want
    cz[z] = want
    lane = lax.broadcasted_iota(I32, (16, 128), 1)
    row = lax.broadcasted_iota(I32, (16, 128), 0)
    some = lax.dot_general(
        jnp.where(lane == z * 16 + row, 1.0, 0.0).astype(BF16), iemb[...], NT,
        preferred_element_type=F32,
    )
    for blk in range(16):
        relay[pl.ds(blk * 16, 16), :] = some[:, blk * 128 : blk * 128 + 128]
    for q in range(NEAR):
        xs[q] = jnp.concatenate(
            [relay[pl.ds(q * 2 + e, 16, stride=16), :] for e in range(2)], axis=1
        ).astype(BF16)
    ds[...] = lax.rsqrt(ideg[...].astype(F32))

    for name in ("rows", "slots", "mask"):
        brought[name].wait()
    cell = slots[...] * 8 + rows[...]
    where = jnp.where(lax.broadcasted_iota(I32, (64, 32), 0) == cell, 1.0, 0.0).astype(BF16)
    lines = mask.reshape(32 * 128, 128)

    def add_blocks(first, last):
        @pl.loop(first, last)
        def _(group):
            for step in range(8):
                i = group * 8 + step
                line = lines[pl.ds(i, 32, stride=128), :].astype(F32).astype(BF16)
                sums = jnp.dot(where, line, preferred_element_type=F32)
                wide_mat[pl.ds(i, 64, stride=128), :] = sums

    add_blocks(0, 8)

    pl.semaphore_wait(barrier, NZ - 1 + NEAR - 1 + 6)

    own_x = pltpu.make_async_copy(xs.at[near], xr.at[near], x_sem.at[1])
    own_x.start()
    own_d = pltpu.make_async_copy(ds, dr.at[near], d_sem.at[1])
    own_d.start()

    @pl.loop(1, NEAR)
    def _(k):
        j_to, slot, there = to_holder(k)
        remote(xs.at[slot], xr.at[there], x_sem.at[0], x_sem.at[1], (z, j_to))
        remote(ds, dr.at[there], d_sem.at[0], d_sem.at[1], (z, j_to))

    @pl.loop(1, NZ)
    def _(k):
        remote(cs, cz.at[z], c_sem.at[0], c_sem.at[1], ((z + k) % NZ, j))

    each_plane_peer(vouch)
    add_blocks(8, 16)
    await_bytes(xr, x_sem.at[1])
    await_bytes(dr, d_sem.at[1])
    i0[...] = xr[...].astype(F32).reshape(128, 256)
    one_scale = dr[...].reshape(128, 128)
    scale_i[...] = jnp.concatenate([one_scale, one_scale], axis=1)
    push_items(0, i0[...])

    await_bytes(cz.at[pl.ds(0, NZ - 1)], c_sem.at[1])
    own_c = pltpu.make_async_copy(cz, cr.at[near], e_sem.at[1])
    own_c.start()

    @pl.loop(1, NEAR)
    def _(k):
        j_to, _, there = to_holder(k)
        remote(cz, cr.at[there], e_sem.at[0], e_sem.at[1], (z, j_to))

    for f in range(8):
        mat[:, f * 128 : f * 128 + 128] = wide_mat[pl.ds(f * 1024, 1024), :].astype(BF16)
    eye = jnp.where(
        lax.broadcasted_iota(I32, (128, 128), 0) == lax.broadcasted_iota(I32, (128, 128), 1), 1.0, 0.0
    ).astype(BF16)
    brought["uemb"].wait()
    brought["udeg"].wait()
    user_rows = lax.dot_general(eye, uemb[...], NT, preferred_element_type=F32)
    u0[...] = user_rows
    scale_u[...] = lax.rsqrt(udeg[...].astype(F32))
    pack_terms(0, to_columns((scale_u[...] * user_rows).astype(BF16)))
    pl.semaphore_wait(entered, NEAR - 1 + 6)
    to_holders_start(0)

    await_bytes(cr, e_sem.at[1])
    col = jnp.stack([cr[:, k] for k in range(NZ)], axis=0).reshape(PEERS, 1, 128)
    x_of = lax.shift_right_logical(col, jnp.full_like(col, 5)) & 3
    y_of = lax.shift_right_logical(col, jnp.full_like(col, 7))
    r_of, p_of = y_of * nc + x_of * c, x_of * nc + y_of * c
    place = (((r_of - r + 4) & 3) * 128 + p_of * 32 + (col & 31)).astype(F32)
    mine = (lax.broadcasted_iota(I32, (8, 128), 1) & 7) == lax.broadcasted_iota(I32, (8, 128), 0)
    spot = jnp.sum(
        jnp.where(mine[None], jnp.broadcast_to(place, (PEERS, 8, 128)), 0.0), axis=2, keepdims=True
    ) * (1.0 / 16.0)
    spot = jnp.broadcast_to(spot, (PEERS, 8, 128)).reshape(512, 128)
    for q in range(4):
        sel[:, q * 128 : q * 128 + 128] = jnp.where(
            spot == (lax.broadcasted_iota(I32, (512, 128), 1) + q * 128).astype(F32), 1.0, 0.0
        ).astype(BF16)
        turned = spot[q * 128 : q * 128 + 128].T
        for m in range(4):
            selt[m * 128 : m * 128 + 128, q * 128 : q * 128 + 128] = jnp.where(
                turned == (lax.broadcasted_iota(I32, (128, 128), 0) + m * 128).astype(F32), 1.0, 0.0
            ).astype(BF16)

    send_picks(1, 0)
    brought["picks"].wait()
    build_picks(0)
    rs_start(0, 0)
    user_one = scale_u[...] * to_users(fetched(1))
    send_terms(2, to_columns((scale_u[...] * user_one).astype(BF16)))
    ufin[...] = u0[...] + user_one
    build_picks(1)
    item_one = scale_i[...] * rs_end(0)
    isum[...] = i0[...] + item_one
    push_items(1, item_one)

    rs_start(1, 2)
    send_picks(3, 1)
    item_final = (isum[...] + scale_i[...] * rs_end(1)) / 3.0
    tables[2, pl.ds(0, 128), :] = item_final.astype(BF16)
    ag_start(2)
    build_picks(2)
    send_picks(4, 2)
    build_picks(3)
    ufin[...] = (ufin[...] + scale_u[...] * to_users(fetched(3))) / 3.0

    final = fetched(4)
    exps = []
    for k in range(4):
        rows = jnp.dot(final, oh[:, k * 1024 : k * 1024 + 1024], preferred_element_type=F32)
        picked[k] = rows
        exps.append(jnp.exp(jnp.sum(ufin[...] * rows, axis=0, keepdims=True)))
    total = exps[0] + exps[1] + exps[2] + exps[3]
    slopes = [e / total - (1.0 if k == 0 else 0.0) for k, e in enumerate(exps)]
    exact = jnp.concatenate([slope * ufin[...] for slope in slopes], axis=1)
    high = exact.astype(BF16)
    low = (exact - high.astype(F32)).astype(BF16)
    spread = lax.dot_general(
        jnp.concatenate([high, low], axis=0), oh[...], NT, preferred_element_type=F32
    )
    send_terms(5, spread[:128] + spread[128:])
    grad = slopes[0] * picked[0]
    for k in range(1, 4):
        grad = grad + slopes[k] * picked[k]
    grad = grad / 3.0
    gu[...] = grad
    down_terms = to_columns((scale_u[...] * grad).astype(BF16))

    rs_start(2, 5)
    send_terms(6, down_terms)
    item_down = rs_end(2) / 3.0
    push_items(3, item_down)
    gi[...] = item_down
    send_picks(7, 3)
    rs_start(3, 6)
    first_item = scale_i[...] * rs_end(3)
    push_items(4, first_item)
    gi[...] = gi[...] + first_item
    first_user = scale_u[...] * to_users(fetched(7))
    send_terms(8, to_columns((scale_u[...] * first_user).astype(BF16)))
    gu[...] = gu[...] + first_user
    send_picks(9, 4)
    rs_start(4, 8)
    out_s[...] = (gi[...] + scale_i[...] * rs_end(4)).astype(BF16)
    own_o = pltpu.make_async_copy(
        out_s.at[pl.ds(pl.multiple_of(near * 16, 16), 16)], out_r.at[me], o_recv.at[2]
    )
    own_o.start()

    def out_step(z_to, k, arrival):
        j_to, slot = to_user(k)
        rows = pl.ds(pl.multiple_of(slot * 16, 16), 16)
        remote(out_s.at[rows], out_r.at[me], o_send.at[0], o_recv.at[arrival], (z_to, j_to))

    for d, arrival in ((2, 0), (6, 1), (1, 2), (7, 2)):

        @pl.loop(0, NEAR)
        def _(k):
            out_step((z + d) % NZ, k, arrival)

    @pl.loop(1, NEAR)
    def _(k):
        out_step(z, k, 2)

    def hand_on(d_from, first, count, d_to, sent, arrival):
        part = out_r.at[pl.ds((z + d_from) % NZ * NEAR + first, count)]
        remote(part, part, o_send.at[sent], o_recv.at[arrival], ((z + d_to) % NZ, j))

    def turn(d_from, first=0, count=NEAR):
        start = (z + d_from) % NZ * NEAR + first

        @pl.loop(0, count)
        def _(k):
            rows = out_r[start + k].astype(F32)
            for e in range(2):
                gi_out[pl.ds((start + k) * 2 + e, 16, stride=128), :] = rows[:, e * 128 : e * 128 + 128]

    await_bytes(out_r.at[pl.ds(0, 8)], o_recv.at[0])
    hand_on(6, 0, 8, 1, 1, 3)
    hand_on(6, 0, 4, 2, 2, 4)
    await_bytes(out_r.at[pl.ds(0, 8)], o_recv.at[1])
    hand_on(2, 0, 8, 7, 3, 5)
    hand_on(2, 4, 4, 6, 4, 6)
    gu_out[...] = gu[...] + scale_u[...] * to_users(fetched(9))
    turn(6)
    turn(2)
    await_bytes(out_r.at[pl.ds(0, 24)], o_recv.at[2])
    for d in (0, 1, 7):
        turn(d)
    await_bytes(out_r.at[pl.ds(0, 8)], o_recv.at[3])
    turn(5)
    await_bytes(out_r.at[pl.ds(0, 8)], o_recv.at[5])
    turn(3)
    await_bytes(out_r.at[pl.ds(0, 4)], o_recv.at[4])
    turn(4, 0, 4)
    await_bytes(out_r.at[pl.ds(0, 4)], o_recv.at[6])
    turn(4, 4, 4)

    await_bytes(xs.at[pl.ds(0, NEAR - 1)], x_sem.at[0])
    await_bytes(dr.at[pl.ds(0, NEAR - 1)], d_sem.at[0])
    await_bytes(cz.at[pl.ds(0, NZ - 1)], c_sem.at[0])
    await_bytes(cr.at[pl.ds(0, NEAR - 1)], e_sem.at[0])
    await_bytes(out_r.at[pl.ds(0, 39)], o_send.at[0])
    for sent, count in ((1, 8), (2, 4), (3, 8), (4, 4)):
        await_bytes(out_r.at[pl.ds(0, count)], o_send.at[sent])
    for n in range(10):
        await_bytes(zs.at[n, pl.ds(0, PEERS - 1)], z_send.at[n])
    for n in range(5):
        await_bytes(tables.at[n, pl.ds(128, 384)], ag_send.at[n])
        await_bytes(rb[n], rs_send.at[n])


def on_device(
    user_emb, item_emb, user_deg, item_deg, blk_rows, blk_slot, fetch_cols, blk_mask, samples
):
    hbm = pl.BlockSpec(memory_space=pltpu.HBM)
    vmem = pl.BlockSpec(memory_space=pltpu.VMEM)
    dma = pltpu.SemaphoreType.DMA
    state = pltpu.VMEM((128, 256), F32)
    users = pltpu.VMEM((128, 1024), F32)
    gu_t, gi_t = pl.pallas_call(
        main_kernel,
        out_shape=(
            jax.ShapeDtypeStruct((128, 1024), F32),
            jax.ShapeDtypeStruct((2048, 128), F32),
        ),
        in_specs=[hbm] * 9,
        out_specs=(vmem, vmem),
        scratch_shapes=[
            users, pltpu.VMEM((1, 1024), F32), state, state, users, users, state, state,
            pltpu.VMEM((1024, 4096), BF16), pltpu.VMEM((4, 128, 1024), F32),
            pltpu.VMEM((512, 512), BF16), pltpu.VMEM((512, 512), BF16),
            pltpu.VMEM((5, 512, 256), BF16),
            pltpu.VMEM((10, PEERS, 16, 128), BF16), pltpu.VMEM((10, PEERS, 16, 128), BF16),
            pltpu.VMEM((1, 128), I32), pltpu.VMEM((NZ, 1, 128), I32), pltpu.VMEM((NEAR, NZ, 1, 128), I32),
            pltpu.VMEM((NEAR, 16, 256), BF16), pltpu.VMEM((NEAR, 16, 256), BF16),
            pltpu.VMEM((16, 128), F32), pltpu.VMEM((NEAR, 16, 128), F32),
            pltpu.VMEM((1024, 128), F32),
            pltpu.VMEM((8192, 128), F32), pltpu.VMEM((1024, 1024), BF16),
            pltpu.VMEM((1, 8), I32), pltpu.VMEM((1024, 128), BF16), pltpu.VMEM((2048, 128), BF16),
            pltpu.VMEM((1, 1024), I32), pltpu.VMEM((16, 128), I32), pltpu.VMEM((4, 1024), I32),
            pltpu.VMEM((1, 32), I32), pltpu.VMEM((1, 32), I32), pltpu.VMEM((32, 128, 128), I32),
            pltpu.VMEM((2, 128, 256), F32),
            *[pltpu.VMEM((3, 128, 256), t) for t in RS_TYPES],
            *[pltpu.VMEM((3, 128, 256), t) for t in RS_TYPES],
            pltpu.VMEM((128, 256), BF16), pltpu.VMEM((PEERS, 16, 256), BF16),
            dma((10,)), dma((10,)), dma((2,)), dma((2,)), dma((2,)), dma((2,)),
            dma((5,)), dma((5,)), dma((5,)), dma((5,)), dma((5,)), dma((7,)), dma((9,)), pltpu.SemaphoreType.REGULAR,
        ],
        compiler_params=pltpu.CompilerParams(
            collective_id=0, has_side_effects=True, vmem_limit_bytes=56 * 2**20
        ),
        name="gcn",
    )(
        fetch_cols.reshape(1, -1), user_emb, item_emb, user_deg.reshape(1, -1), item_deg.reshape(16, 128),
        samples.T, blk_rows.reshape(1, -1), blk_slot.reshape(1, -1), blk_mask,
    )
    return pl.pallas_call(
        finish_kernel,
        out_shape=(
            jax.ShapeDtypeStruct((1024, 128), F32),
            jax.ShapeDtypeStruct((2048, 128), F32),
        ),
        in_specs=[pl.BlockSpec(memory_space=pl.ANY)] * 2,
        out_specs=(pl.BlockSpec(memory_space=pl.ANY), pl.BlockSpec(memory_space=pl.ANY)),
        scratch_shapes=[
            users, pltpu.VMEM((2048, 128), F32), pltpu.VMEM((1024, 128), F32),
            pltpu.VMEM((2048, 128), F32), dma((5,)), dma((5,)),
        ],
        compiler_params=pltpu.CompilerParams(vmem_limit_bytes=56 * 2**20),
        name="finish",
    )(gu_t, gi_t)


def solution(mesh):
    both = ("ugrp", "item")
    return jax.shard_map(
        on_device,
        mesh=mesh,
        in_specs=(
            P(both, None), P("item", None), P(both), P("item"), P(both), P(both), P(both),
            P(both, None, None), P(both, None),
        ),
        out_specs=(P(both, None), P("item", None)),
        check_vma=False,
    )
```

```python
import jax
import jax.numpy as jnp
from jax import lax
from jax.experimental import pallas as pl
from jax.experimental.pallas import tpu as pltpu
from jax.sharding import PartitionSpec as P

F32, BF16, I32 = jnp.float32, jnp.bfloat16, jnp.int32
MESH = pl.DeviceIdType.MESH
NT = (((1,), (1,)), ((), ()))
NZ, PEERS, NEAR = 8, 64, 8
RS_TYPES = (BF16, BF16, F32, BF16, BF16)


def finish_kernel(gu_in, gi_in, gu_out, gi_out, gu_t, gi_t, gu, gi, came, left):
    parts = [pl.ds(i * 512, 512) for i in range(4)]
    loads = [pltpu.make_async_copy(gi_in.at[p], gi_t.at[p], came.at[i]) for i, p in enumerate(parts)]
    loads.append(pltpu.make_async_copy(gu_in, gu_t, came.at[4]))
    stores = [pltpu.make_async_copy(gi.at[p], gi_out.at[p], left.at[i]) for i, p in enumerate(parts)]
    stores.append(pltpu.make_async_copy(gu, gu_out, left.at[4]))
    for load in loads:
        load.start()
    for i in range(4):
        loads[i].wait()
        for blk in range(4):
            rows = pl.ds(i * 512 + blk * 128, 128)
            gi[rows, :] = gi_t[rows, :].T
        stores[i].start()
    loads[4].wait()
    gu[...] = gu_t[...].T
    stores[4].start()
    for store in stores:
        store.wait()


def main_kernel(
    cols_in, uemb_in, iemb_in, udeg_in, ideg_in, picks_in, rows_in, slots_in, mask_in,
    gu_out, gi_out,
    u0, scale_u, i0, scale_i, ufin, gu, gi, isum,
    oh, picked, sel, selt, tables, zs, zr, cs, cz, cr, xs, xr, ds, dr, relay, wide_mat, mat,
    cols, uemb, iemb, udeg, ideg, picks, rows, slots, mask,
    pf, sb0, sb1, sb2, sb3, sb4, rb0, rb1, rb2, rb3, rb4, out_s, out_r,
    z_send, z_recv, c_sem, e_sem, x_sem, d_sem, ag_send, ag_recv, rs_send, rs_recv, o_send, o_recv, m_sem, entered,
):
    sb, rb = (sb0, sb1, sb2, sb3, sb4), (rb0, rb1, rb2, rb3, rb4)
    z, j = lax.axis_index("ugrp"), lax.axis_index("item")
    c = j % 2
    x, y = (j // 2) % 4, j // 8
    nc = 1 - c
    p, r = x * nc + y * c, y * nc + x * c
    near = p * 2 + c
    me = z * NEAR + near

    def device(x_to, y_to, c_to):
        return (y_to * 4 + x_to) * 2 + c_to

    def along(d):
        r_to = (r + d) % 4
        return (z, device(p * nc + r_to * c, r_to * nc + p * c, c))

    def offset(k):
        return (p + k // 2) % 4, (c + k % 2) % 2

    def plane(i):
        return (z + 4 + ((i + 1) // 2) * (1 - 2 * (i % 2))) % NZ

    def to_user(k):
        p_to, c_to = offset(k)
        return device(p_to * nc + x * c, y * nc + p_to * c, c_to), p_to * 2 + c_to

    def to_holder(k):
        p_to, c_to = offset(k)
        j_to = device(p_to * (1 - c_to) + x * c_to, y * (1 - c_to) + p_to * c_to, c_to)
        return j_to, p_to * 2 + c_to, (x * (1 - c_to) + y * c_to) * 2 + c

    def remote(src, dst, send, recv, to):
        pltpu.make_async_remote_copy(
            src_ref=src, dst_ref=dst, send_sem=send, recv_sem=recv, device_id=to, device_id_type=MESH
        ).start()

    def await_bytes(ref, sem):
        pltpu.make_async_copy(ref, ref, sem).wait()

    brought = {}
    for n, (name, src, dst) in enumerate((
        ("iemb", iemb_in, iemb), ("ideg", ideg_in, ideg), ("cols", cols_in, cols),
        ("uemb", uemb_in, uemb), ("udeg", udeg_in, udeg), ("rows", rows_in, rows),
        ("slots", slots_in, slots), ("mask", mask_in, mask), ("picks", picks_in, picks),
    )):
        brought[name] = pltpu.make_async_copy(src, dst, m_sem.at[n])
        brought[name].start()
    barrier = pltpu.get_barrier_semaphore()

    def greet(to):
        pl.semaphore_signal(barrier, inc=1, device_id=to, device_id_type=MESH)

    @pl.loop(1, NZ)
    def _(k):
        greet(((z + k) % NZ, j))

    def each_plane_peer(signal):
        for d in (1, 2, 3):
            signal(along(d))
            signal((z, device((x + d * c) % 4, (y + d * nc) % 4, nc)))

        @pl.loop(1, NEAR)
        def _(k):
            signal((z, to_user(k)[0]))

    each_plane_peer(greet)

    def vouch(to):
        pl.semaphore_signal(entered, inc=1, device_id=to, device_id_type=MESH)

    def own_start(n):
        own = pltpu.make_async_copy(zs.at[n, me], zr.at[n, me], z_recv.at[n])
        own.start()

    def to_users_start(n):
        own_start(n)

        @pl.loop(0, PEERS - 1)
        def _(k):
            z_to = plane(k // NEAR)
            j_to, slot = to_user(NEAR - 1 - k % NEAR)
            remote(
                zs.at[n, z_to * NEAR + slot], zr.at[n, me], z_send.at[n], z_recv.at[n], (z_to, j_to)
            )

    def to_holders_start(n):
        own_start(n)

        @pl.loop(0, PEERS - 1)
        def _(k):
            z_to = plane(k // NEAR)
            j_to, slot, there = to_holder(NEAR - 1 - k % NEAR)
            remote(
                zs.at[n, z_to * NEAR + slot], zr.at[n, z * NEAR + there],
                z_send.at[n], z_recv.at[n], (z_to, j_to),
            )

    def z_wait(n):
        await_bytes(zr.at[n], z_recv.at[n])

    def ag_start(n):
        for d in (2, 1, 3):
            remote(
                tables.at[n, pl.ds(0, 128)], tables.at[n, pl.ds((4 - d) * 128, 128)],
                ag_send.at[n], ag_recv.at[n], along(d),
            )

    def ag_wait(n):
        await_bytes(tables.at[n, pl.ds(128, 384)], ag_recv.at[n])

    def rs_start(n, zn):
        z_wait(zn)
        got = zr[zn].astype(F32)
        terms = jnp.concatenate(
            [got[:, :8].reshape(512, 128), got[:, 8:].reshape(512, 128)], axis=1
        ).astype(BF16)
        for d in (2, 1, 3, 0):
            part = jnp.dot(selt[pl.ds(d * 128, 128), :], terms, preferred_element_type=F32)
            if d:
                sb[n][d - 1] = part.astype(sb[n].dtype)
                remote(sb[n].at[d - 1], rb[n].at[d - 1], rs_send.at[n], rs_recv.at[n], along(d))
            else:
                pf[n % 2] = part

    def rs_end(n):
        await_bytes(rb[n], rs_recv.at[n])
        return pf[n % 2] + rb[n][0].astype(F32) + rb[n][1].astype(F32) + rb[n][2].astype(F32)

    def pack_terms(zn, terms):
        for f in range(8):
            relay[pl.ds(f, 128, stride=8), :] = terms[:, f * 128 : f * 128 + 128]
        zs[zn] = relay[...].reshape(PEERS, 16, 128).astype(BF16)

    def send_terms(zn, terms):
        pack_terms(zn, terms)
        to_holders_start(zn)

    def send_picks(zn, n):
        ag_wait(n)
        found = jnp.dot(sel[...], tables[n], preferred_element_type=F32)
        zs[zn] = jnp.concatenate(
            [found[:, :128].reshape(PEERS, 8, 128), found[:, 128:].reshape(PEERS, 8, 128)], axis=1
        ).astype(BF16)
        to_users_start(zn)

    def fetched(zn):
        z_wait(zn)
        relay[...] = zr[zn].astype(F32).reshape(1024, 128)
        return jnp.concatenate(
            [relay[pl.ds(f, 128, stride=8), :] for f in range(8)], axis=1
        ).astype(BF16)

    def to_users(rows):
        return lax.dot_general(rows, mat[...], NT, preferred_element_type=F32)

    def to_columns(rows):
        return jnp.dot(rows, mat[...], preferred_element_type=F32)

    def push_items(n, rows):
        tables[n, pl.ds(0, 128), :] = (scale_i[...] * rows).astype(BF16)
        ag_start(n)

    def build_picks(k):
        line = picks[pl.ds(k, 1), :]

        @pl.loop(0, 8)
        def _(r):
            at_row = pl.multiple_of(r * 128, 128)
            number = lax.broadcasted_iota(I32, (128, 1024), 0) + at_row
            oh[pl.ds(at_row, 128), k * 1024 : k * 1024 + 1024] = jnp.where(number == line, 1.0, 0.0).astype(BF16)

    for name in ("cols", "iemb", "ideg"):
        brought[name].wait()
    lane_row = lax.broadcasted_iota(I32, (1, 128), 1) & 7
    want = jnp.zeros((1, 128), I32)
    for f in range(8):
        want = jnp.where(lane_row == f, cols[:, f : f + 1], want)
    cs[...] = want
    cz[z] = want
    lane = lax.broadcasted_iota(I32, (16, 128), 1)
    row = lax.broadcasted_iota(I32, (16, 128), 0)
    some = lax.dot_general(
        jnp.where(lane == z * 16 + row, 1.0, 0.0).astype(BF16), iemb[...], NT,
        preferred_element_type=F32,
    )
    for blk in range(16):
        relay[pl.ds(blk * 16, 16), :] = some[:, blk * 128 : blk * 128 + 128]
    for q in range(NEAR):
        xs[q] = jnp.concatenate(
            [relay[pl.ds(q * 2 + e, 16, stride=16), :] for e in range(2)], axis=1
        ).astype(BF16)
    ds[...] = lax.rsqrt(ideg[...].astype(F32))

    for name in ("rows", "slots", "mask"):
        brought[name].wait()
    cell = slots[...] * 8 + rows[...]
    where = jnp.where(lax.broadcasted_iota(I32, (64, 32), 0) == cell, 1.0, 0.0).astype(BF16)
    lines = mask.reshape(32 * 128, 128)

    def add_blocks(first, last):
        @pl.loop(first, last)
        def _(group):
            for step in range(8):
                i = group * 8 + step
                line = lines[pl.ds(i, 32, stride=128), :].astype(F32).astype(BF16)
                sums = jnp.dot(where, line, preferred_element_type=F32)
                wide_mat[pl.ds(i, 64, stride=128), :] = sums

    add_blocks(0, 8)

    pl.semaphore_wait(barrier, NZ - 1 + NEAR - 1 + 6)

    own_x = pltpu.make_async_copy(xs.at[near], xr.at[near], x_sem.at[1])
    own_x.start()
    own_d = pltpu.make_async_copy(ds, dr.at[near], d_sem.at[1])
    own_d.start()

    @pl.loop(1, NEAR)
    def _(k):
        j_to, slot, there = to_holder(k)
        remote(xs.at[slot], xr.at[there], x_sem.at[0], x_sem.at[1], (z, j_to))
        remote(ds, dr.at[there], d_sem.at[0], d_sem.at[1], (z, j_to))

    @pl.loop(1, NZ)
    def _(k):
        remote(cs, cz.at[z], c_sem.at[0], c_sem.at[1], ((z + k) % NZ, j))

    each_plane_peer(vouch)
    add_blocks(8, 16)
    await_bytes(xr, x_sem.at[1])
    await_bytes(dr, d_sem.at[1])
    i0[...] = xr[...].astype(F32).reshape(128, 256)
    one_scale = dr[...].reshape(128, 128)
    scale_i[...] = jnp.concatenate([one_scale, one_scale], axis=1)
    push_items(0, i0[...])

    await_bytes(cz.at[pl.ds(0, NZ - 1)], c_sem.at[1])
    own_c = pltpu.make_async_copy(cz, cr.at[near], e_sem.at[1])
    own_c.start()

    @pl.loop(1, NEAR)
    def _(k):
        j_to, _, there = to_holder(k)
        remote(cz, cr.at[there], e_sem.at[0], e_sem.at[1], (z, j_to))

    for f in range(8):
        mat[:, f * 128 : f * 128 + 128] = wide_mat[pl.ds(f * 1024, 1024), :].astype(BF16)
    eye = jnp.where(
        lax.broadcasted_iota(I32, (128, 128), 0) == lax.broadcasted_iota(I32, (128, 128), 1), 1.0, 0.0
    ).astype(BF16)
    brought["uemb"].wait()
    brought["udeg"].wait()
    user_rows = lax.dot_general(eye, uemb[...], NT, preferred_element_type=F32)
    u0[...] = user_rows
    scale_u[...] = lax.rsqrt(udeg[...].astype(F32))
    pack_terms(0, to_columns((scale_u[...] * user_rows).astype(BF16)))
    pl.semaphore_wait(entered, NEAR - 1 + 6)
    to_holders_start(0)

    await_bytes(cr, e_sem.at[1])
    col = jnp.stack([cr[:, k] for k in range(NZ)], axis=0).reshape(PEERS, 1, 128)
    x_of = lax.shift_right_logical(col, jnp.full_like(col, 5)) & 3
    y_of = lax.shift_right_logical(col, jnp.full_like(col, 7))
    r_of, p_of = y_of * nc + x_of * c, x_of * nc + y_of * c
    place = (((r_of - r + 4) & 3) * 128 + p_of * 32 + (col & 31)).astype(F32)
    mine = (lax.broadcasted_iota(I32, (8, 128), 1) & 7) == lax.broadcasted_iota(I32, (8, 128), 0)
    spot = jnp.sum(
        jnp.where(mine[None], jnp.broadcast_to(place, (PEERS, 8, 128)), 0.0), axis=2, keepdims=True
    ) * (1.0 / 16.0)
    spot = jnp.broadcast_to(spot, (PEERS, 8, 128)).reshape(512, 128)
    for q in range(4):
        sel[:, q * 128 : q * 128 + 128] = jnp.where(
            spot == (lax.broadcasted_iota(I32, (512, 128), 1) + q * 128).astype(F32), 1.0, 0.0
        ).astype(BF16)
        turned = spot[q * 128 : q * 128 + 128].T
        for m in range(4):
            selt[m * 128 : m * 128 + 128, q * 128 : q * 128 + 128] = jnp.where(
                turned == (lax.broadcasted_iota(I32, (128, 128), 0) + m * 128).astype(F32), 1.0, 0.0
            ).astype(BF16)

    send_picks(1, 0)
    brought["picks"].wait()
    build_picks(0)
    rs_start(0, 0)
    item_one = scale_i[...] * rs_end(0)
    isum[...] = i0[...] + item_one
    push_items(1, item_one)
    user_one = scale_u[...] * to_users(fetched(1))
    send_terms(2, to_columns((scale_u[...] * user_one).astype(BF16)))
    ufin[...] = u0[...] + user_one
    build_picks(1)

    rs_start(1, 2)
    send_picks(3, 1)
    item_final = (isum[...] + scale_i[...] * rs_end(1)) / 3.0
    tables[2, pl.ds(0, 128), :] = item_final.astype(BF16)
    ag_start(2)
    build_picks(2)
    send_picks(4, 2)
    build_picks(3)
    ufin[...] = (ufin[...] + scale_u[...] * to_users(fetched(3))) / 3.0

    final = fetched(4)
    exps = []
    for k in range(4):
        rows = jnp.dot(final, oh[:, k * 1024 : k * 1024 + 1024], preferred_element_type=F32)
        picked[k] = rows
        exps.append(jnp.exp(jnp.sum(ufin[...] * rows, axis=0, keepdims=True)))
    total = exps[0] + exps[1] + exps[2] + exps[3]
    slopes = [e / total - (1.0 if k == 0 else 0.0) for k, e in enumerate(exps)]
    exact = jnp.concatenate([slope * ufin[...] for slope in slopes], axis=1)
    high = exact.astype(BF16)
    low = (exact - high.astype(F32)).astype(BF16)
    spread = lax.dot_general(
        jnp.concatenate([high, low], axis=0), oh[...], NT, preferred_element_type=F32
    )
    send_terms(5, spread[:128] + spread[128:])
    grad = slopes[0] * picked[0]
    for k in range(1, 4):
        grad = grad + slopes[k] * picked[k]
    grad = grad / 3.0
    gu[...] = grad
    down_terms = to_columns((scale_u[...] * grad).astype(BF16))

    rs_start(2, 5)
    send_terms(6, down_terms)
    item_down = rs_end(2) / 3.0
    push_items(3, item_down)
    gi[...] = item_down
    send_picks(7, 3)
    rs_start(3, 6)
    first_item = scale_i[...] * rs_end(3)
    push_items(4, first_item)
    gi[...] = gi[...] + first_item
    first_user = scale_u[...] * to_users(fetched(7))
    send_terms(8, to_columns((scale_u[...] * first_user).astype(BF16)))
    gu[...] = gu[...] + first_user
    send_picks(9, 4)
    rs_start(4, 8)
    out_s[...] = (gi[...] + scale_i[...] * rs_end(4)).astype(BF16)
    own_o = pltpu.make_async_copy(
        out_s.at[pl.ds(pl.multiple_of(near * 16, 16), 16)], out_r.at[me], o_recv.at[2]
    )
    own_o.start()

    def out_step(z_to, k, arrival):
        j_to, slot = to_user(k)
        rows = pl.ds(pl.multiple_of(slot * 16, 16), 16)
        remote(out_s.at[rows], out_r.at[me], o_send.at[0], o_recv.at[arrival], (z_to, j_to))

    for d, arrival in ((2, 0), (6, 1), (1, 2), (7, 2)):

        @pl.loop(0, NEAR)
        def _(k):
            out_step((z + d) % NZ, k, arrival)

    @pl.loop(1, NEAR)
    def _(k):
        out_step(z, k, 2)

    def hand_on(d_from, first, count, d_to, sent, arrival):
        part = out_r.at[pl.ds((z + d_from) % NZ * NEAR + first, count)]
        remote(part, part, o_send.at[sent], o_recv.at[arrival], ((z + d_to) % NZ, j))

    def turn(d_from, first=0, count=NEAR):
        start = (z + d_from) % NZ * NEAR + first

        @pl.loop(0, count, unroll=4)
        def _(k):
            rows = out_r[start + k].astype(F32)
            for e in range(2):
                gi_out[pl.ds((start + k) * 2 + e, 16, stride=128), :] = rows[:, e * 128 : e * 128 + 128]

    await_bytes(out_r.at[pl.ds(0, 8)], o_recv.at[0])
    hand_on(6, 0, 8, 1, 1, 3)
    hand_on(6, 0, 4, 2, 2, 4)
    await_bytes(out_r.at[pl.ds(0, 8)], o_recv.at[1])
    hand_on(2, 0, 8, 7, 3, 5)
    hand_on(2, 4, 4, 6, 4, 6)
    gu_out[...] = gu[...] + scale_u[...] * to_users(fetched(9))
    turn(6)
    turn(2)
    await_bytes(out_r.at[pl.ds(0, 24)], o_recv.at[2])
    for d in (0, 1, 7):
        turn(d)
    await_bytes(out_r.at[pl.ds(0, 8)], o_recv.at[3])
    turn(5)
    await_bytes(out_r.at[pl.ds(0, 8)], o_recv.at[5])
    turn(3)
    await_bytes(out_r.at[pl.ds(0, 4)], o_recv.at[4])
    turn(4, 0, 4)
    await_bytes(out_r.at[pl.ds(0, 4)], o_recv.at[6])
    turn(4, 4, 4)

    await_bytes(xs.at[pl.ds(0, NEAR - 1)], x_sem.at[0])
    await_bytes(dr.at[pl.ds(0, NEAR - 1)], d_sem.at[0])
    await_bytes(cz.at[pl.ds(0, NZ - 1)], c_sem.at[0])
    await_bytes(cr.at[pl.ds(0, NEAR - 1)], e_sem.at[0])
    await_bytes(out_r.at[pl.ds(0, 39)], o_send.at[0])
    for sent, count in ((1, 8), (2, 4), (3, 8), (4, 4)):
        await_bytes(out_r.at[pl.ds(0, count)], o_send.at[sent])
    for n in range(10):
        await_bytes(zs.at[n, pl.ds(0, PEERS - 1)], z_send.at[n])
    for n in range(5):
        await_bytes(tables.at[n, pl.ds(128, 384)], ag_send.at[n])
        await_bytes(rb[n], rs_send.at[n])


def on_device(
    user_emb, item_emb, user_deg, item_deg, blk_rows, blk_slot, fetch_cols, blk_mask, samples
):
    hbm = pl.BlockSpec(memory_space=pltpu.HBM)
    vmem = pl.BlockSpec(memory_space=pltpu.VMEM)
    dma = pltpu.SemaphoreType.DMA
    state = pltpu.VMEM((128, 256), F32)
    users = pltpu.VMEM((128, 1024), F32)
    gu_t, gi_t = pl.pallas_call(
        main_kernel,
        out_shape=(
            jax.ShapeDtypeStruct((128, 1024), F32),
            jax.ShapeDtypeStruct((2048, 128), F32),
        ),
        in_specs=[hbm] * 9,
        out_specs=(vmem, vmem),
        scratch_shapes=[
            users, pltpu.VMEM((1, 1024), F32), state, state, users, users, state, state,
            pltpu.VMEM((1024, 4096), BF16), pltpu.VMEM((4, 128, 1024), F32),
            pltpu.VMEM((512, 512), BF16), pltpu.VMEM((512, 512), BF16),
            pltpu.VMEM((5, 512, 256), BF16),
            pltpu.VMEM((10, PEERS, 16, 128), BF16), pltpu.VMEM((10, PEERS, 16, 128), BF16),
            pltpu.VMEM((1, 128), I32), pltpu.VMEM((NZ, 1, 128), I32), pltpu.VMEM((NEAR, NZ, 1, 128), I32),
            pltpu.VMEM((NEAR, 16, 256), BF16), pltpu.VMEM((NEAR, 16, 256), BF16),
            pltpu.VMEM((16, 128), F32), pltpu.VMEM((NEAR, 16, 128), F32),
            pltpu.VMEM((1024, 128), F32),
            pltpu.VMEM((8192, 128), F32), pltpu.VMEM((1024, 1024), BF16),
            pltpu.VMEM((1, 8), I32), pltpu.VMEM((1024, 128), BF16), pltpu.VMEM((2048, 128), BF16),
            pltpu.VMEM((1, 1024), I32), pltpu.VMEM((16, 128), I32), pltpu.VMEM((4, 1024), I32),
            pltpu.VMEM((1, 32), I32), pltpu.VMEM((1, 32), I32), pltpu.VMEM((32, 128, 128), I32),
            pltpu.VMEM((2, 128, 256), F32),
            *[pltpu.VMEM((3, 128, 256), t) for t in RS_TYPES],
            *[pltpu.VMEM((3, 128, 256), t) for t in RS_TYPES],
            pltpu.VMEM((128, 256), BF16), pltpu.VMEM((PEERS, 16, 256), BF16),
            dma((10,)), dma((10,)), dma((2,)), dma((2,)), dma((2,)), dma((2,)),
            dma((5,)), dma((5,)), dma((5,)), dma((5,)), dma((5,)), dma((7,)), dma((9,)), pltpu.SemaphoreType.REGULAR,
        ],
        compiler_params=pltpu.CompilerParams(
            collective_id=0, has_side_effects=True, vmem_limit_bytes=56 * 2**20
        ),
        name="gcn",
    )(
        fetch_cols.reshape(1, -1), user_emb, item_emb, user_deg.reshape(1, -1), item_deg.reshape(16, 128),
        samples.T, blk_rows.reshape(1, -1), blk_slot.reshape(1, -1), blk_mask,
    )
    return pl.pallas_call(
        finish_kernel,
        out_shape=(
            jax.ShapeDtypeStruct((1024, 128), F32),
            jax.ShapeDtypeStruct((2048, 128), F32),
        ),
        in_specs=[pl.BlockSpec(memory_space=pl.ANY)] * 2,
        out_specs=(pl.BlockSpec(memory_space=pl.ANY), pl.BlockSpec(memory_space=pl.ANY)),
        scratch_shapes=[
            users, pltpu.VMEM((2048, 128), F32), pltpu.VMEM((1024, 128), F32),
            pltpu.VMEM((2048, 128), F32), dma((5,)), dma((5,)),
        ],
        compiler_params=pltpu.CompilerParams(vmem_limit_bytes=56 * 2**20),
        name="finish",
    )(gu_t, gi_t)


def solution(mesh):
    both = ("ugrp", "item")
    return jax.shard_map(
        on_device,
        mesh=mesh,
        in_specs=(
            P(both, None), P("item", None), P(both), P("item"), P(both), P(both), P(both),
            P(both, None, None), P(both, None),
        ),
        out_specs=(P(both, None), P("item", None)),
        check_vma=False,
    )
```
